512 devices in a mesh: blk: 128 (over x, z, core), gz: 4 (over y).
Axes of the slice: x: 4, y: 4, z: 16, core: 2. Of those that a mesh axis runs over, the one named last changes fastest.
Arguments:
- fixed: bfloat16 [128, 32, 32, 128], P('blk', 'gz'), may hold values from -6 to 6
- moving: bfloat16 [128, 32, 32, 128], P('blk', 'gz'), may hold values from -6 to 6
- block_place: int32 [128], P('blk'), may hold values from 0 to 127, each once
- tissue: int32 [128], P('blk'), may hold values 0 or 1
Outputs:
- velocity: float32 [3, 2, 32, 64], replicated
- cc_map: float32 [128, 32, 32, 128], P('blk', 'gz')
The draws below stay inside these ranges and needn't reach their ends.
Inputs may be any that keep to these rules, and one draw needn't show every extreme that they name: `block_place`: each block position from 0 to 127 is named by exactly one block.
All inputs are finite; a program needn't handle non-finite values. No bound on the sum of `tissue` on one device may be relied on, other than what follows from the above.
Results may differ from the reference program's by a relative error of at most 0.0004.
Values may be sent and summed in bfloat16 or wider, within the bound.
A program may use at most 64 MiB of HBM per device.

```python
import math
import jax
import jax.numpy as jnp
from jax import lax

BX = 32
BY = 128
SCALE = 16
GY = 8
ITERS = 2
BLOCKS = 128
GX = 16
NZ = 32
CZD = 2
CX = 2
CY = 8


def with_ends(result, own_key, smallest, high):
    shape = result.shape
    spot = [jax.random.randint(jax.random.fold_in(own_key, axis), (), 0, shape[axis]) for axis in range(len(shape))]
    result = result.at[tuple(spot)].set(smallest)
    longest = shape.index(max(shape))
    spot[longest] = (spot[longest] + 1) % shape[longest]
    return result.at[tuple(spot)].set(high)


def shard_levels(key, extent, shards, least, high):
    factor_of = 1.0
    for dim, shards_of in shards:
        draws = jax.random.uniform(jax.random.fold_in(jax.random.fold_in(key, 6), dim), (shards_of,), jnp.float32, least / len(shards), high / len(shards))
        factor_of = factor_of * jnp.repeat(jnp.exp(draws), extent[dim] // shards_of).reshape((-1,) + (1,) * (len(extent) - 1 - dim))
    return factor_of


def gaussian(rng, dims, scale, bound, cuts=(), held_as=jnp.bfloat16):
    loudness = shard_levels(rng, dims, cuts, -0.22, 0.18) if cuts else 1.0
    drawn = jax.random.normal(rng, dims, jnp.float32) * scale * loudness
    return jnp.minimum(jnp.maximum(drawn, -bound), bound).astype(held_as)


def setup_inputs(seed: int = 0) -> dict:
    keys = jax.random.split(jax.random.key(seed), 5)
    return {
        "fixed": gaussian(keys[0], (BLOCKS, NZ, BX, BY), 1.0, 6.0, ((0, 128), (1, 4))),
        "moving": gaussian(keys[1], (BLOCKS, NZ, BX, BY), 1.0, 6.0, ((0, 128), (1, 4))),
        "block_place": jax.random.permutation(keys[2], BLOCKS).astype(jnp.int32),
        "tissue": with_ends((jax.random.randint(keys[3], (BLOCKS,), 0, 5) < 3).astype(jnp.int32), jax.random.fold_in(keys[3], 1), 0, 1),
    }


EXACT = lax.Precision.HIGHEST
EPSILON = 1e-05
STEP_LENGTH = 0.5
BOX_TAPS = [1.0 / 9.0] * 9
GAUSS_RAW = [math.exp(-(offset - 3) ** 2 / 4.5) for offset in range(7)]
GAUSS_TAPS = [value / sum(GAUSS_RAW) for value in GAUSS_RAW]

def tap_matrix(count, taps):
    radius = len(taps) // 2
    rows = jnp.arange(count)[:, None]
    cols = jnp.arange(count)[None, :]
    matrix = jnp.zeros((count, count), jnp.float32)
    for offset, weight in enumerate(taps):
        matrix = matrix + weight * (rows - cols == offset - radius).astype(jnp.float32)
    return matrix

def along_rows(field, matrix):
    return jnp.einsum('...xy,xu->...uy', field, matrix, precision=EXACT)

def along_cols(field, matrix):
    return jnp.einsum('...y,yv->...v', field, matrix, precision=EXACT)

def planes_filter(field, taps, count):
    total = jnp.zeros(field.shape[:-3] + (count,) + field.shape[-2:], jnp.float32)
    for offset, weight in enumerate(taps):
        total = total + weight * field[..., offset:offset + count, :, :]
    return total

def slope(field, axis):
    widths = [(0, 0)] * field.ndim
    widths[axis] = (1, 1)
    padded = jnp.pad(field, widths)
    length = field.shape[axis]
    upper = lax.slice_in_dim(padded, 2, length + 2, axis=axis)
    lower = lax.slice_in_dim(padded, 0, length, axis=axis)
    return 0.5 * (upper - lower)

def hat_rows(coords, count):
    where = jnp.clip((coords + 0.5) / SCALE - 0.5, 0.0, count - 1.0)
    marks = jnp.arange(count).astype(jnp.float32)
    return jnp.maximum(0.0, 1.0 - jnp.abs(where[..., None] - marks))

def statistics(means, fixed_c, warped_c):
    sii = means[2] - means[0] * means[0]
    sww = means[3] - means[1] * means[1]
    siw = means[4] - means[0] * means[1]
    denom = sii * sww + EPSILON
    similar = siw * siw / denom
    weight = 2.0 * siw / denom * (fixed_c - means[0] - siw / (sww + EPSILON) * (warped_c - means[1]))
    return (similar, weight)

def smooth_axis(field, axis):
    widths = [(0, 0)] * field.ndim
    widths[axis] = (1, 1)
    padded = jnp.pad(field, widths)
    length = field.shape[axis]
    upper = lax.slice_in_dim(padded, 2, length + 2, axis=axis)
    lower = lax.slice_in_dim(padded, 0, length, axis=axis)
    return 0.25 * lower + 0.5 * field + 0.25 * upper

def regularize(velocity, total, coarse_rows, coarse_cols):
    block_rows = velocity.shape[2] // coarse_rows
    coarse_depth = velocity.shape[1]
    grid = total.reshape(block_rows, GY, 3, coarse_depth, coarse_rows, coarse_cols)
    grid = grid.transpose(2, 3, 0, 4, 1, 5).reshape(velocity.shape)
    regular = smooth_axis(smooth_axis(smooth_axis(grid, 1), 2), 3)
    return velocity + STEP_LENGTH * regular / jnp.sqrt(jnp.mean(regular * regular) + EPSILON)

def block_step(fixed_b, moving_b, place_b, tissue_b, velocity, box_rows, box_cols, gauss_rows, gauss_cols):
    image_i = fixed_b.astype(jnp.float32)
    image_j = moving_b.astype(jnp.float32)
    block_row = place_b // GY
    block_col = place_b % GY
    row_hat = hat_rows((block_row * BX + jnp.arange(BX)).astype(jnp.float32), GX * CX)
    col_hat = hat_rows((block_col * BY + jnp.arange(BY)).astype(jnp.float32), GY * CY)
    depth_hat = hat_rows(jnp.arange(NZ).astype(jnp.float32), CZD)
    partial_value = jnp.einsum('ckab,xa->ckxb', velocity, row_hat, precision=EXACT)
    partial_value = jnp.einsum('ckxb,yb->ckxy', partial_value, col_hat, precision=EXACT)
    shift = jnp.einsum('zk,ckxy->czxy', depth_hat, partial_value, precision=EXACT)
    warped = image_j + shift[0] * slope(image_j, 0) + shift[1] * slope(image_j, 1) + shift[2] * slope(image_j, 2)
    fields = jnp.stack([image_i, warped, image_i * image_i, warped * warped, image_i * warped], 0)
    padded = jnp.pad(fields, ((0, 0), (4, 4), (0, 0), (0, 0)))
    means = planes_filter(padded, BOX_TAPS, NZ)
    means = along_cols(along_rows(means, box_rows), box_cols)
    similar, weight = statistics(means, image_i, warped)
    scale = weight * tissue_b.astype(jnp.float32)
    force = jnp.stack([scale * slope(warped, 0), scale * slope(warped, 1), scale * slope(warped, 2)], 0)
    padded = jnp.pad(force, ((0, 0), (3, 3), (0, 0), (0, 0)))
    smooth = planes_filter(padded, GAUSS_TAPS, NZ)
    smooth = along_cols(along_rows(smooth, gauss_rows), gauss_cols)
    piece = smooth.reshape(3, CZD, SCALE, CX, SCALE, CY, SCALE).sum(axis=(2, 4, 6))
    return (piece, similar)

def reference(fixed, moving, block_place, tissue):
    box_rows = tap_matrix(BX, BOX_TAPS)
    box_cols = tap_matrix(BY, BOX_TAPS)
    gauss_rows = tap_matrix(BX, GAUSS_TAPS)
    gauss_cols = tap_matrix(BY, GAUSS_TAPS)
    velocity = jnp.zeros((3, CZD, GX * CX, GY * CY), jnp.float32)
    positions = jnp.arange(BLOCKS)
    onehot = (positions[:, None] == block_place[None, :]).astype(jnp.float32)
    correlation = jnp.zeros((BLOCKS, NZ, BX, BY), jnp.float32)
    for rounds in range(ITERS):

        def one_block(items):
            return block_step(items[0], items[1], items[2], items[3], velocity, box_rows, box_cols, gauss_rows, gauss_cols)
        pieces, correlation = lax.map(one_block, (fixed, moving, block_place, tissue))
        total = jnp.dot(onehot, pieces.reshape(BLOCKS, -1), precision=EXACT)
        velocity = regularize(velocity, total, CX, CY)
    return (velocity, correlation)
```

```python
import functools
import math

import jax
import jax.numpy as jnp
from jax import lax
from jax.experimental import pallas as pl
from jax.experimental.pallas import tpu as pltpu
from jax.sharding import PartitionSpec as P

NX, NY, NZC = 4, 4, 16
F32, BF16 = jnp.float32, jnp.bfloat16
EPSILON = 1e-05
STEP_LENGTH = 0.5
RAW = [math.exp(-(t * t) / 4.5) for t in range(4)]
TOTAL = RAW[0] + 2 * (RAW[1] + RAW[2] + RAW[3])
W1, W2, W3 = (RAW[t] / TOTAL for t in (1, 2, 3))
PLACE_LANE = 48
MESH = pl.DeviceIdType.MESH


def coordinates():
    blk = lax.axis_index("blk")
    return blk // (2 * NZC), lax.axis_index("gz"), (blk // 2) % NZC, blk % 2


def device(x, y, z, core):
    return ((x * NZC + z) * 2 + core, y)


def peers():
    x, y, z, core = coordinates()
    along_y = [device(x, (y + d) % NY, z, core) for d in range(1, NY)]
    along_z = [device(x, y, (z + d) % NZC, core) for d in range(1, NZC)]
    along_x = [device((x + d // 2) % NX, y, z, (core + d) % 2) for d in range(1, 2 * NX)]
    return along_y, along_z, along_x


def iota(shape, dim):
    return lax.broadcasted_iota(jnp.int32, shape, dim)


def split(value):
    high = value.astype(BF16)
    return high, (value - high.astype(F32)).astype(BF16)


def group_weight(t):
    near = jnp.minimum(t, 15 - t)
    out = jnp.where(near >= 3, 1.0, 0.0)
    for at, value in (
        (2, 1 - W3),
        (1, 1 - W3 - W2),
        (0, 1 - W3 - W2 - W1),
        (-1, W1 + W2 + W3),
        (-2, W2 + W3),
        (-3, W3),
    ):
        out = jnp.where(near == at, value, out)
    return out


def hat_tri(where, mark):
    gap = where - mark
    hat = lambda d: jnp.maximum(0.0, 1.0 - jnp.abs(d))
    return 0.5 * hat(gap) + 0.25 * (hat(gap - 1.0) + hat(gap + 1.0))


def window_sums(planes):
    two = [planes[i] + planes[i + 1] for i in range(15)]
    four = [two[i] + two[i + 2] for i in range(13)]
    eight = [four[i] + four[i + 4] for i in range(8)]
    return [eight[i] + planes[i + 8] for i in range(8)]


def shifted(value, amount, dim):
    size = value.shape[dim]
    at = iota(value.shape, dim)
    edge = 0 if amount == 1 else size - 1
    return jnp.where(at == edge, 0.0, pltpu.roll(value, amount % size, dim))


def kernel(
    fixed_hbm, moving_hbm, place_ref, tissue_ref,
    velocity_ref, cc_hbm,
    own_i, own_j, halo_i, halo_j,
    image_i, image_j, slope_x, slope_y, warped_ref,
    box_rows, box_cols, grad_rows, grad_cols, gauss_cols, spread,
    sums, means, stat_i, cc_ref, expanded,
    rows_y, rows_z, local_sem, halo_send, halo_recv, gather_send, gather_recv,
):
    x, y, z, core = coordinates()
    gz = y
    along_y, along_z, along_x = peers()
    barrier = pltpu.get_barrier_semaphore()
    for peer in along_y + along_z + along_x:
        pl.semaphore_signal(barrier, inc=1, device_id=peer, device_id_type=MESH)
    load_i = pltpu.make_async_copy(fixed_hbm.at[0], own_i, local_sem.at[0])
    load_j = pltpu.make_async_copy(moving_hbm.at[0], own_j, local_sem.at[1])
    load_i.start()
    load_j.start()

    r, c = iota((256, 256), 0), iota((256, 256), 1)
    same = (r >> 5) == (c >> 5)
    box_rows[...] = jnp.where(same & (jnp.abs(r - c) <= 4), 1.0, 0.0).astype(BF16)
    grad_rows[...] = jnp.where(
        same & (c - r == 1), 0.5, jnp.where(same & (r - c == 1), -0.5, 0.0)
    ).astype(BF16)
    r, c = iota((128, 128), 0), iota((128, 128), 1)
    band = jnp.where(jnp.abs(r - c) <= 4, 1.0, 0.0).astype(BF16)
    box_cols[0:128, :] = band
    box_cols[128:256, :] = band
    grad_cols[...] = jnp.where(r - c == 1, 0.5, jnp.where(c - r == 1, -0.5, 0.0)).astype(BF16)
    high, low = split(group_weight(r - 16 * (c & 7)))
    gauss_cols[0:128, :] = high
    gauss_cols[128:256, :] = high
    gauss_cols[256:384, :] = low
    r, c = iota((128, 768), 0), iota((128, 768), 1)
    half = jnp.where(c >= 384, 1, 0)
    c = c - 384 * half
    pick = ((r >> 6) == half) & (((r >> 3) & 7) == (c >> 6)) & ((r & 7) == (c & 7))
    pick = jnp.where(pick, 1.0, 0.0).astype(BF16)
    spread[0:128, :] = pick
    spread[128:256, :] = pick

    load_i.wait()
    load_j.wait()
    pl.semaphore_wait(barrier, len(along_y) + len(along_z) + len(along_x))

    up, down = along_y[0], along_y[2]
    halos = []
    for index, (source, target, peer) in enumerate(
        (
            (own_j.at[3:8], halo_j.at[0], up),
            (own_j.at[0:5], halo_j.at[1], down),
            (own_i.at[4:8], halo_i.at[0], up),
            (own_i.at[0:4], halo_i.at[1], down),
        )
    ):
        copy = pltpu.make_async_remote_copy(
            source, target, halo_send.at[index], halo_recv.at[index],
            device_id=peer, device_id_type=MESH,
        )
        copy.start()
        halos.append(copy)

    inside_low = jnp.where(gz > 0, 1.0, 0.0)
    inside_high = jnp.where(gz < NY - 1, 1.0, 0.0)
    for p in range(8):
        image_i[4 + p] = own_i[p].astype(F32)
        image_j[5 + p] = own_j[p].astype(F32)
    flat = own_j[...].reshape(256, 128)
    slope_x[128:384, :] = jnp.dot(grad_rows[...], flat, preferred_element_type=F32)
    slope_y[128:384, :] = jnp.dot(flat, grad_cols[...], preferred_element_type=F32)

    for copy in halos:
        copy.wait_recv()
    for p in range(5):
        image_j[p] = halo_j[0, p].astype(F32) * inside_low
        image_j[13 + p] = halo_j[1, p].astype(F32) * inside_high
    for p in range(4):
        image_i[p] = halo_i[0, p].astype(F32) * inside_low
        image_i[12 + p] = halo_i[1, p].astype(F32) * inside_high

    def box_sums(slot):
        field = jnp.dot(box_rows[...], sums[slot], preferred_element_type=F32)
        high, low = split(field[:, :128] + field[:, 128:])
        field = jnp.dot(high, box_cols[0:128, :], preferred_element_type=F32) + jnp.dot(
            low, box_cols[0:128, :], preferred_element_type=F32
        )
        return field * (1.0 / 729.0)

    def put_sums(slot, chunk, planes):
        for p, value in enumerate(window_sums(planes)):
            high, low = split(value)
            at = pl.ds(32 * p + 16 * chunk, 16)
            sums[slot, at, 0:128] = high
            sums[slot, at, 128:256] = low

    depth_weight = []
    for p in range(8):
        at = gz * 8 + p
        first = group_weight(at)
        second = group_weight(at - 16)
        depth_weight.append((0.5 * first + 0.25 * second, 0.25 * first + 0.5 * second))
    lane = iota((32, 128), 1)
    lane_group = (lane >> 3) & 7
    row_weight = group_weight(iota((32, 128), 0) - 16 * (lane >> 6))
    place = place_ref[0]
    tissue = tissue_ref[0].astype(F32)

    def piece(planes, first):
        totals = [None] * 6
        for p in range(8):
            at = pl.ds(32 * p, 32)
            mean_i, var_i = stat_i[0, at, :], stat_i[1, at, :]
            mean_w = means[0, at, :]
            var_w = means[1, at, :] - mean_w * mean_w
            cov = means[2, at, :] - mean_i * mean_w
            denom = var_i * var_w + EPSILON
            ratio = cov / denom
            if not first:
                cc_ref[p] = cov * ratio
            image = image_i[4 + p]
            mid = planes[4 + p]
            dcc = 2.0 * ratio * (image - mean_i - cov / (var_w + EPSILON) * (mid - mean_w))
            if first:
                along_rows = slope_x[128 + 32 * p : 160 + 32 * p, :]
                along_cols = slope_y[128 + 32 * p : 160 + 32 * p, :]
            else:
                along_rows = 0.5 * (shifted(mid, -1, 0) - shifted(mid, 1, 0))
                along_cols = 0.5 * (shifted(mid, -1, 1) - shifted(mid, 1, 1))
            along_depth = 0.5 * (planes[5 + p] - planes[3 + p])
            for c, slope in enumerate((along_depth, along_rows, along_cols)):
                force = dcc * slope
                for k in range(2):
                    term = depth_weight[p][k] * force
                    totals[2 * c + k] = term if p == 0 else totals[2 * c + k] + term
        merged = jnp.zeros((32, 128), F32)
        for ck in range(6):
            high, low = split(totals[ck])
            part = (
                jnp.dot(high, gauss_cols[0:128, :], preferred_element_type=F32)
                + jnp.dot(low, gauss_cols[0:128, :], preferred_element_type=F32)
                + jnp.dot(high, gauss_cols[256:384, :], preferred_element_type=F32)
            )
            merged = jnp.where(lane_group == ck, part, merged)
        row = jnp.sum(merged * row_weight, axis=0, keepdims=True) * tissue
        lane_row = iota((1, 128), 1)
        return jnp.where(lane_row == PLACE_LANE, place.astype(F32) * 0.25, row)

    unsent = []

    def exchange(source, targets, everything, sem, partners):
        for d, peer in enumerate(partners):
            pltpu.make_async_remote_copy(
                source, targets(d + 1), gather_send.at[sem], gather_recv.at[sem],
                device_id=peer, device_id_type=MESH,
            ).start()
        done = pltpu.make_async_remote_copy(
            everything, everything, gather_send.at[sem], gather_recv.at[sem],
            device_id=partners[0], device_id_type=MESH,
        )
        done.wait_recv()
        unsent.append(done)

    def gather(turn, row):
        one, many = rows_y.at[turn], rows_z.at[turn]
        rows_y[turn, 0] = row
        exchange(one.at[0], lambda d: one.at[d], one.at[1:NY], 3 * turn, along_y)
        rows_z[turn, 0, 0] = (rows_y[turn, 0] + rows_y[turn, 2]) + (
            rows_y[turn, 1] + rows_y[turn, 3]
        )
        exchange(
            many.at[0, 0], lambda d: many.at[0, d], many.at[0, 1:NZC], 3 * turn + 1, along_z
        )
        exchange(many.at[0], lambda d: many.at[d], many.at[1 : 2 * NX], 3 * turn + 2, along_x)
        return rows_z[turn].reshape(128, 128)

    for chunk in range(2):
        at = pl.ds(16 * chunk, 16)
        fixed = [image_i[p, at, :] for p in range(16)]
        put_sums(0, chunk, fixed)
        put_sums(1, chunk, [value * value for value in fixed])
        moved = [image_j[1 + p, at, :] for p in range(16)]
        put_sums(2, chunk, moved)
        put_sums(3, chunk, [value * value for value in moved])
        put_sums(4, chunk, [a * b for a, b in zip(fixed, moved)])
    mean_i = box_sums(0)
    stat_i[0] = mean_i
    stat_i[1] = box_sums(1) - mean_i * mean_i
    for slot in range(3):
        means[slot] = box_sums(2 + slot)
    row = piece([image_j[1 + p] for p in range(16)], True)
    gathered = gather(0, row)

    for start, side, offset in ((0, 0, 1), (384, 1, 0)):
        flat = halo_j[side, offset : offset + 4].reshape(128, 128)
        slope_x[start : start + 128, :] = jnp.dot(
            grad_rows[0:128, 0:128], flat, preferred_element_type=F32
        )
        slope_y[start : start + 128, :] = jnp.dot(
            flat, grad_cols[...], preferred_element_type=F32
        )

    spot = jnp.broadcast_to(gathered[:, PLACE_LANE : PLACE_LANE + 1], (128, 128)).astype(jnp.int32)
    r, c = iota((128, 128), 0), iota((128, 128), 1)
    in_column = (spot & 7) == ((c >> 3) & 7)
    spot_row = jnp.sum(jnp.where(r == c, spot, 0).astype(F32), axis=0, keepdims=True).astype(
        jnp.int32
    )
    mark = ((spot_row >> 3) * 2).astype(F32)
    mark = jnp.broadcast_to(jnp.concatenate([mark, mark + 1.0], axis=1), (64, 256))
    at = iota((64, 256), 0)
    own_row, own_col = place >> 3, place & 7
    inner = (own_row * 32 + at - 32).astype(F32)
    inner = jnp.clip((inner + 0.5) * (1.0 / 16.0) - 0.5, 0.0, 31.0)
    where = jnp.where(at < 32, at.astype(F32), inner)
    combine = hat_tri(where, mark).astype(BF16)
    r, c = iota((128, 256), 0), iota((128, 256), 1)
    inner = (own_col * 128 + (c & 127)).astype(F32)
    inner = jnp.clip((inner + 0.5) * (1.0 / 16.0) - 0.5, 0.0, 63.0)
    to_cols = jnp.where(
        (r >> 6) == (c >> 7), hat_tri(inner, (r & 63).astype(F32)), 0.0
    ).astype(BF16)

    def grid_of(gathered, count):
        high, low = split(gathered)
        wide = jnp.dot(high, spread[0:128, :], preferred_element_type=F32) + jnp.dot(
            low, spread[0:128, :], preferred_element_type=F32
        )
        for tile in range(6):
            value = jnp.where(in_column, wide[:, 128 * tile : 128 * tile + 128], 0.0)
            high, low = split(value)
            at = 128 * (tile // 3)
            lanes = pl.ds(128 * (tile % 3), 128)
            expanded[at : at + 128, lanes] = high
            expanded[256 + at : 384 + at, lanes] = low
        left = combine[0:count]
        return jnp.dot(left, expanded[0:256, :], preferred_element_type=F32) + jnp.dot(
            left, expanded[256:512, :], preferred_element_type=F32
        )

    def regular_of(grid):
        out = []
        at = iota((32, 128), 1) & 63
        squares = jnp.zeros((32, 128), F32)
        for tile in range(3):
            value = grid[:, 128 * tile : 128 * tile + 128]
            left = jnp.where(at == 0, 0.0, pltpu.roll(value, 1, 1))
            right = jnp.where(at == 63, 0.0, pltpu.roll(value, 127, 1))
            value = 0.5 * value + 0.25 * (left + right)
            squares = squares + value * value
            out.append(value)
        mean = jnp.sum(squares, keepdims=True) * (1.0 / (6 * 32 * 64))
        return out, STEP_LENGTH / jnp.sqrt(mean + EPSILON)

    grid = grid_of(gathered, 64)
    regular, scale = regular_of(grid[0:32])
    before = [value * scale for value in regular]
    shift = []
    for tile in range(3):
        high, low = split(grid[32:64, 128 * tile : 128 * tile + 128])
        value = jnp.dot(high, to_cols, preferred_element_type=F32) + jnp.dot(
            low, to_cols, preferred_element_type=F32
        )
        value = value * scale
        shift.append((value[:, :128], value[:, 128:] - value[:, :128]))

    for p in range(16):
        deep = (gz * 8 + (p - 4)).astype(F32)
        part = jnp.clip((deep + 0.5) * (1.0 / 16.0) - 0.5, 0.0, 1.0)
        value = image_j[1 + p]
        slopes = (
            0.5 * (image_j[2 + p] - image_j[p]),
            slope_x[32 * p : 32 * p + 32, :],
            slope_y[32 * p : 32 * p + 32, :],
        )
        for (base, rise), slope in zip(shift, slopes):
            value = value + (base + part * rise) * slope
        if p < 4:
            value = value * inside_low
        if p >= 12:
            value = value * inside_high
        warped_ref[p] = value
    for chunk in range(2):
        at = pl.ds(16 * chunk, 16)
        moved = [warped_ref[p, at, :] for p in range(16)]
        put_sums(2, chunk, moved)
        put_sums(3, chunk, [value * value for value in moved])
        put_sums(4, chunk, [image_i[p, at, :] * value for p, value in enumerate(moved)])
    for slot in range(3):
        means[slot] = box_sums(2 + slot)
    row = piece([warped_ref[p] for p in range(16)], False)
    store = pltpu.make_async_copy(cc_ref, cc_hbm.at[0], local_sem.at[0])
    store.start()
    gathered = gather(1, row)
    regular, scale = regular_of(grid_of(gathered, 32))
    for tile in range(3):
        value = before[tile] + regular[tile] * scale
        velocity_ref[tile, 0] = value[:, 0:64]
        velocity_ref[tile, 1] = value[:, 64:128]
    for copy in halos:
        copy.wait_send()
    for copy in unsent:
        copy.wait_send()
    store.wait()


def per_device(fixed, moving, block_place, tissue):
    vmem = pltpu.VMEM
    return pl.pallas_call(
        kernel,
        out_shape=(
            jax.ShapeDtypeStruct((3, 2, 32, 64), F32),
            jax.ShapeDtypeStruct((1, 8, 32, 128), F32),
        ),
        in_specs=[
            pl.BlockSpec(memory_space=pl.ANY),
            pl.BlockSpec(memory_space=pl.ANY),
            pl.BlockSpec(memory_space=pltpu.SMEM),
            pl.BlockSpec(memory_space=pltpu.SMEM),
        ],
        out_specs=(
            pl.BlockSpec(memory_space=pltpu.VMEM),
            pl.BlockSpec(memory_space=pl.ANY),
        ),
        scratch_shapes=[
            vmem((8, 32, 128), BF16),
            vmem((8, 32, 128), BF16),
            vmem((2, 4, 32, 128), BF16),
            vmem((2, 5, 32, 128), BF16),
            vmem((16, 32, 128), F32),
            vmem((18, 32, 128), F32),
            vmem((512, 128), F32),
            vmem((512, 128), F32),
            vmem((16, 32, 128), F32),
            vmem((256, 256), BF16),
            vmem((256, 128), BF16),
            vmem((256, 256), BF16),
            vmem((128, 128), BF16),
            vmem((384, 128), BF16),
            vmem((256, 768), BF16),
            vmem((5, 256, 256), BF16),
            vmem((3, 256, 128), F32),
            vmem((2, 256, 128), F32),
            vmem((8, 32, 128), F32),
            vmem((512, 384), BF16),
            vmem((2, NY, 1, 128), F32),
            vmem((2, 2 * NX, NZC, 1, 128), F32),
            pltpu.SemaphoreType.DMA((2,)),
            pltpu.SemaphoreType.DMA((4,)),
            pltpu.SemaphoreType.DMA((4,)),
            pltpu.SemaphoreType.DMA((6,)),
            pltpu.SemaphoreType.DMA((6,)),
        ],
        compiler_params=pltpu.CompilerParams(
            collective_id=0, has_side_effects=True, vmem_limit_bytes=32 * 1024 * 1024
        ),
    )(fixed, moving, block_place, tissue)


def solution(mesh):
    return jax.shard_map(
        per_device,
        mesh=mesh,
        in_specs=(P("blk", "gz", None, None), P("blk", "gz", None, None), P("blk"), P("blk")),
        out_specs=(P(), P("blk", "gz", None, None)),
        check_vma=False,
    )
```

```python
import functools
import math

import jax
import jax.numpy as jnp
from jax import lax
from jax.experimental import pallas as pl
from jax.experimental.pallas import tpu as pltpu
from jax.sharding import PartitionSpec as P

NX, NY, NZC = 4, 4, 16
F32, BF16 = jnp.float32, jnp.bfloat16
EPSILON = 1e-05
STEP_LENGTH = 0.5
RAW = [math.exp(-(t * t) / 4.5) for t in range(4)]
TOTAL = RAW[0] + 2 * (RAW[1] + RAW[2] + RAW[3])
W1, W2, W3 = (RAW[t] / TOTAL for t in (1, 2, 3))
PLACE_LANE = 48
MESH = pl.DeviceIdType.MESH


def coordinates():
    blk = lax.axis_index("blk")
    return blk // (2 * NZC), lax.axis_index("gz"), (blk // 2) % NZC, blk % 2


def device(x, y, z, core):
    return ((x * NZC + z) * 2 + core, y)


def far_first():
    steps = [(z, x, c) for z in range(NZC) for x in range(NX) for c in range(2)][1:]
    return sorted(steps, key=lambda s: -(min(s[0], NZC - s[0]) + min(s[1], NX - s[1]) + 0.3 * s[2]))


def peers():
    x, y, z, core = coordinates()
    along_y = [device(x, (y + d) % NY, z, core) for d in range(1, NY)]
    along_x = [device((x + d // 2) % NX, y, z, (core + d) % 2) for d in range(1, 2 * NX)]
    along_z = {d: device(x, y, (z + d) % NZC, core) for d in (1, 2, 3, 6, 10, 13, 14, 15)}
    others = [
        device((x + dx) % NX, y, (z + dz) % NZC, (core + dc) % 2) for dz, dx, dc in far_first()
    ]
    return along_y, along_x, along_z, others


def iota(shape, dim):
    return lax.broadcasted_iota(jnp.int32, shape, dim)


def split(value):
    high = value.astype(BF16)
    return high, (value - high.astype(F32)).astype(BF16)


def group_weight(t):
    near = jnp.minimum(t, 15 - t)
    out = jnp.where(near >= 3, 1.0, 0.0)
    for at, value in (
        (2, 1 - W3),
        (1, 1 - W3 - W2),
        (0, 1 - W3 - W2 - W1),
        (-1, W1 + W2 + W3),
        (-2, W2 + W3),
        (-3, W3),
    ):
        out = jnp.where(near == at, value, out)
    return out


def hat_tri(where, mark):
    gap = where - mark
    hat = lambda d: jnp.maximum(0.0, 1.0 - jnp.abs(d))
    return 0.5 * hat(gap) + 0.25 * (hat(gap - 1.0) + hat(gap + 1.0))


def own_sums(a):
    mid = a[3] + a[4]
    out0 = (a[0] + a[1]) + (a[2] + mid)
    out1 = out0 + a[5]
    out2 = out1 + a[6]
    out3 = out2 + a[7]
    out7 = mid + (a[5] + (a[6] + a[7]))
    out6 = out7 + a[2]
    out5 = out6 + a[1]
    return [out0, out1, out2, out3, out3, out5, out6, out7]


def side_sums(low, high):
    out3 = low[3]
    out2 = low[2] + out3
    out1 = low[1] + out2
    out0 = low[0] + out1
    out4 = high[0]
    out5 = out4 + high[1]
    out6 = out5 + high[2]
    out7 = out6 + high[3]
    return [out0, out1, out2, out3, out4, out5, out6, out7]


def shifted(value, amount, dim):
    size = value.shape[dim]
    at = iota(value.shape, dim)
    edge = 0 if amount == 1 else size - 1
    return jnp.where(at == edge, 0.0, pltpu.roll(value, amount % size, dim))


def kernel(
    fixed_hbm, moving_hbm, place_ref, tissue_ref,
    velocity_ref, cc_hbm,
    own_i, own_j, halo_i, halo_j,
    image_i, image_j, slope_x, slope_y, warped_ref,
    box_rows, box_cols, grad_rows, grad_cols, gauss_cols, spread,
    inner_sums, sums, means, stat_i, cc_ref, expanded, cols_twice,
    rows_y, rows, local_sem, halo_send, halo_recv, gather_send, gather_recv, known,
):
    gz = lax.axis_index("gz")
    along_y, along_x, along_z, others = peers()
    near_z = [along_z[d] for d in (1, 2, 3, 13, 14, 15)]
    barrier = pltpu.get_barrier_semaphore()
    for peer in along_y + along_x + near_z:
        pl.semaphore_signal(barrier, inc=1, device_id=peer, device_id_type=MESH)
    load_j = pltpu.make_async_copy(moving_hbm.at[0], own_j, local_sem.at[0])
    load_i = pltpu.make_async_copy(fixed_hbm.at[0], own_i, local_sem.at[1])
    load_j.start()
    load_i.start()
    pl.semaphore_wait(barrier, len(along_y) + len(along_x) + len(near_z))

    up, down = along_y[0], along_y[2]
    halos = []
    for index, (source, target, peer) in enumerate(
        (
            (moving_hbm.at[0, 3:8], halo_j.at[0], up),
            (moving_hbm.at[0, 0:5], halo_j.at[1], down),
            (fixed_hbm.at[0, 4:8], halo_i.at[0], up),
            (fixed_hbm.at[0, 0:4], halo_i.at[1], down),
        )
    ):
        copy = pltpu.make_async_remote_copy(
            source, target, halo_send.at[index], halo_recv.at[index],
            device_id=peer, device_id_type=MESH,
        )
        copy.start()
        halos.append(copy)
    for peer in near_z:
        pl.semaphore_signal(known.at[0], inc=1, device_id=peer, device_id_type=MESH)

    r, c = iota((256, 256), 0), iota((256, 256), 1)
    same = (r >> 5) == (c >> 5)
    box_rows[...] = jnp.where(same & (jnp.abs(r - c) <= 4), 1.0, 0.0).astype(BF16)
    grad_rows[...] = jnp.where(
        same & (c - r == 1), 0.5, jnp.where(same & (r - c == 1), -0.5, 0.0)
    ).astype(BF16)
    r, c = iota((128, 128), 0), iota((128, 128), 1)
    band = jnp.where(jnp.abs(r - c) <= 4, 1.0, 0.0).astype(BF16)
    box_cols[0:128, :] = band
    box_cols[128:256, :] = band
    grad_cols[...] = jnp.where(r - c == 1, 0.5, jnp.where(c - r == 1, -0.5, 0.0)).astype(BF16)
    high, low = split(group_weight(r - 16 * (c & 7)))
    gauss_cols[0:128, :] = high
    gauss_cols[128:256, :] = high
    gauss_cols[256:384, :] = low

    inside_low = jnp.where(gz > 0, 1.0, 0.0)
    inside_high = jnp.where(gz < NY - 1, 1.0, 0.0)
    load_j.wait()
    load_i.wait()
    for p in range(8):
        image_i[4 + p] = own_i[p].astype(F32)
        image_j[5 + p] = own_j[p].astype(F32)
    flat = own_j[...].reshape(256, 128)
    slope_x[128:384, :] = jnp.dot(grad_rows[...], flat, preferred_element_type=F32)
    slope_y[128:384, :] = jnp.dot(flat, grad_cols[...], preferred_element_type=F32)

    def box_sums(slot):
        field = jnp.dot(box_rows[...], sums[slot], preferred_element_type=F32)
        high, low = split(field[:, :128] + field[:, 128:])
        field = jnp.dot(
            jnp.concatenate([high, low], axis=1), box_cols[...], preferred_element_type=F32
        )
        return field * (1.0 / 729.0)

    def products(fixed, moved):
        return (
            fixed,
            [a * a for a in fixed],
            moved,
            [b * b for b in moved],
            [a * b for a, b in zip(fixed, moved)],
        )

    def put_sums(slot, chunk, inner, outer):
        for p in range(8):
            high, low = split(inner[p] + outer[p])
            at = pl.ds(32 * p + 16 * chunk, 16)
            sums[slot, at, 0:128] = high
            sums[slot, at, 128:256] = low

    for chunk in range(2):
        at = pl.ds(16 * chunk, 16)
        fixed = [image_i[4 + p, at, :] for p in range(8)]
        moved = [image_j[5 + p, at, :] for p in range(8)]
        for slot, planes in enumerate(products(fixed, moved)):
            for p, value in enumerate(own_sums(planes)):
                inner_sums[slot, p, at, :] = value

    for copy in halos:
        copy.wait_recv()
    pl.semaphore_wait(known.at[0], len(near_z))
    for d in (6, 10):
        pl.semaphore_signal(known.at[1], inc=1, device_id=along_z[d], device_id_type=MESH)

    for p in range(5):
        image_j[p] = halo_j[0, p].astype(F32) * inside_low
        image_j[13 + p] = halo_j[1, p].astype(F32) * inside_high
    for p in range(4):
        image_i[p] = halo_i[0, p].astype(F32) * inside_low
        image_i[12 + p] = halo_i[1, p].astype(F32) * inside_high

    depth_weight = []
    for p in range(8):
        at = gz * 8 + p
        first = group_weight(at)
        second = group_weight(at - 16)
        depth_weight.append((0.5 * first + 0.25 * second, 0.25 * first + 0.5 * second))
    lane = iota((32, 128), 1)
    lane_group = (lane >> 3) & 7
    row_weight = group_weight(iota((32, 128), 0) - 16 * (lane >> 6))
    place = place_ref[0]
    tissue = tissue_ref[0].astype(F32)

    def piece(planes, first):
        totals = [None] * 6
        for p in range(8):
            at = pl.ds(32 * p, 32)
            mean_i, var_i = stat_i[0, at, :], stat_i[1, at, :]
            mean_w = means[0, at, :]
            var_w = means[1, at, :] - mean_w * mean_w
            cov = means[2, at, :] - mean_i * mean_w
            denom = var_i * var_w + EPSILON
            ratio = cov / denom
            if not first:
                cc_ref[p] = cov * ratio
            image = image_i[4 + p]
            mid = planes[4 + p]
            dcc = 2.0 * ratio * (image - mean_i - cov / (var_w + EPSILON) * (mid - mean_w))
            if first:
                along_rows = slope_x[128 + 32 * p : 160 + 32 * p, :]
                along_cols = slope_y[128 + 32 * p : 160 + 32 * p, :]
            else:
                along_rows = 0.5 * (shifted(mid, -1, 0) - shifted(mid, 1, 0))
                along_cols = 0.5 * (shifted(mid, -1, 1) - shifted(mid, 1, 1))
            along_depth = 0.5 * (planes[5 + p] - planes[3 + p])
            for c, slope in enumerate((along_depth, along_rows, along_cols)):
                force = dcc * slope
                for k in range(2):
                    term = depth_weight[p][k] * force
                    totals[2 * c + k] = term if p == 0 else totals[2 * c + k] + term
        stack = []
        for ck in range(6):
            high, low = split(totals[ck])
            stack.append(jnp.concatenate([high, low, high], axis=1))
        parts = jnp.dot(
            jnp.concatenate(stack, axis=0), gauss_cols[...], preferred_element_type=F32
        )
        merged = jnp.zeros((32, 128), F32)
        for ck in range(6):
            merged = jnp.where(lane_group == ck, parts[32 * ck : 32 * ck + 32], merged)
        row = jnp.sum(merged * row_weight, axis=0, keepdims=True) * tissue
        lane_row = iota((1, 128), 1)
        return jnp.where(lane_row == PLACE_LANE, place.astype(F32) * 0.25, row)

    def exchange(source, targets, everything, sem, partners):
        for d, peer in enumerate(partners):
            pltpu.make_async_remote_copy(
                source, targets.at[d + 1], gather_send.at[sem], gather_recv.at[sem],
                device_id=peer, device_id_type=MESH,
            ).start()
        return pltpu.make_async_remote_copy(
            everything, everything, gather_send.at[sem], gather_recv.at[sem],
            device_id=partners[0], device_id_type=MESH,
        )

    def start_gather(turn, row):
        mine, every = rows_y.at[turn], rows.at[turn]
        rows_y[turn, 0] = row
        done_y = exchange(mine.at[0], mine, mine.at[1:NY], 2 * turn, along_y)
        if turn == 0:
            pl.semaphore_wait(known.at[1], 2)
        done_y.wait_recv()
        rows[turn, 0] = (rows_y[turn, 0] + rows_y[turn, 2]) + (rows_y[turn, 1] + rows_y[turn, 3])
        return done_y, exchange(every.at[0], every, every.at[1:128], 2 * turn + 1, others)

    for chunk in range(2):
        at = pl.ds(16 * chunk, 16)
        fixed = [image_i[p, at, :] for p in (0, 1, 2, 3, 12, 13, 14, 15)]
        moved = [image_j[1 + p, at, :] for p in (0, 1, 2, 3, 12, 13, 14, 15)]
        for slot, planes in enumerate(products(fixed, moved)):
            inner = [inner_sums[slot, p, at, :] for p in range(8)]
            put_sums(slot, chunk, inner, side_sums(planes[:4], planes[4:]))
    mean_i = box_sums(0)
    stat_i[0] = mean_i
    stat_i[1] = box_sums(1) - mean_i * mean_i
    for slot in range(3):
        means[slot] = box_sums(2 + slot)
    row = piece([image_j[1 + p] for p in range(16)], True)
    first_y, first = start_gather(0, row)

    r, c = iota((128, 768), 0), iota((128, 768), 1)
    half = jnp.where(c >= 384, 1, 0)
    c = c - 384 * half
    pick = ((r >> 6) == half) & (((r >> 3) & 7) == (c >> 6)) & ((r & 7) == (c & 7))
    pick = jnp.where(pick, 1.0, 0.0).astype(BF16)
    spread[0:128, :] = pick
    spread[128:256, :] = pick
    own_row, own_col = place >> 3, place & 7
    r, c = iota((128, 256), 0), iota((128, 256), 1)
    inner = (own_col * 128 + (c & 127)).astype(F32)
    inner = jnp.clip((inner + 0.5) * (1.0 / 16.0) - 0.5, 0.0, 63.0)
    to_cols = jnp.where(
        (r >> 6) == (c >> 7), hat_tri(inner, (r & 63).astype(F32)), 0.0
    ).astype(BF16)
    cols_twice[0:128, :] = to_cols
    cols_twice[128:256, :] = to_cols
    for start, side, offset in ((0, 0, 1), (384, 1, 0)):
        flat = halo_j[side, offset : offset + 4].reshape(128, 128)
        slope_x[start : start + 128, :] = jnp.dot(
            grad_rows[0:128, 0:128], flat, preferred_element_type=F32
        )
        slope_y[start : start + 128, :] = jnp.dot(
            flat, grad_cols[...], preferred_element_type=F32
        )

    first.wait_recv()
    gathered = rows[0].reshape(128, 128)

    spot = jnp.broadcast_to(gathered[:, PLACE_LANE : PLACE_LANE + 1], (128, 128)).astype(jnp.int32)
    r, c = iota((128, 128), 0), iota((128, 128), 1)
    in_column = (spot & 7) == ((c >> 3) & 7)
    spot_row = jnp.sum(jnp.where(r == c, spot, 0).astype(F32), axis=0, keepdims=True).astype(
        jnp.int32
    )
    mark = ((spot_row >> 3) * 2).astype(F32)
    mark = jnp.broadcast_to(jnp.concatenate([mark, mark + 1.0], axis=1), (64, 256))
    at = iota((64, 256), 0)
    inner = (own_row * 32 + at - 32).astype(F32)
    inner = jnp.clip((inner + 0.5) * (1.0 / 16.0) - 0.5, 0.0, 31.0)
    where = jnp.where(at < 32, at.astype(F32), inner)
    combine = hat_tri(where, mark).astype(BF16)
    combine = jnp.concatenate([combine, combine], axis=1)

    def grid_of(gathered, count):
        high, low = split(gathered)
        wide = jnp.dot(
            jnp.concatenate([high, low], axis=1), spread[...], preferred_element_type=F32
        )
        for tile in range(6):
            value = jnp.where(in_column, wide[:, 128 * tile : 128 * tile + 128], 0.0)
            high, low = split(value)
            at = 128 * (tile // 3)
            lanes = pl.ds(128 * (tile % 3), 128)
            expanded[at : at + 128, lanes] = high
            expanded[256 + at : 384 + at, lanes] = low
        return jnp.dot(combine[0:count], expanded[...], preferred_element_type=F32)

    def regular_of(grid):
        out = []
        at = iota((32, 128), 1) & 63
        squares = jnp.zeros((32, 128), F32)
        for tile in range(3):
            value = grid[:, 128 * tile : 128 * tile + 128]
            left = jnp.where(at == 0, 0.0, pltpu.roll(value, 1, 1))
            right = jnp.where(at == 63, 0.0, pltpu.roll(value, 127, 1))
            value = 0.5 * value + 0.25 * (left + right)
            squares = squares + value * value
            out.append(value)
        mean = jnp.sum(squares, keepdims=True) * (1.0 / (6 * 32 * 64))
        return out, STEP_LENGTH / jnp.sqrt(mean + EPSILON)

    grid = grid_of(gathered, 64)
    regular, scale = regular_of(grid[0:32])
    before = [value * scale for value in regular]
    stack = []
    for tile in range(3):
        stack.append(
            jnp.concatenate(split(grid[32:64, 128 * tile : 128 * tile + 128]), axis=1)
        )
    moves = scale * jnp.dot(
        jnp.concatenate(stack, axis=0), cols_twice[...], preferred_element_type=F32
    )
    shift = []
    for c in range(3):
        value = moves[32 * c : 32 * c + 32]
        shift.append((value[:, :128], value[:, 128:] - value[:, :128]))

    for p in range(16):
        deep = (gz * 8 + (p - 4)).astype(F32)
        part = jnp.clip((deep + 0.5) * (1.0 / 16.0) - 0.5, 0.0, 1.0)
        value = image_j[1 + p]
        slopes = (
            0.5 * (image_j[2 + p] - image_j[p]),
            slope_x[32 * p : 32 * p + 32, :],
            slope_y[32 * p : 32 * p + 32, :],
        )
        for (base, rise), slope in zip(shift, slopes):
            value = value + (base + part * rise) * slope
        if p < 4:
            value = value * inside_low
        if p >= 12:
            value = value * inside_high
        warped_ref[p] = value
    for chunk in range(2):
        at = pl.ds(16 * chunk, 16)
        fixed = [image_i[p, at, :] for p in range(16)]
        moved = [warped_ref[p, at, :] for p in range(16)]
        for slot, planes in enumerate(products(fixed, moved)):
            if slot >= 2:
                put_sums(
                    slot, chunk, own_sums(planes[4:12]), side_sums(planes[0:4], planes[12:16])
                )
    for slot in range(3):
        means[slot] = box_sums(2 + slot)
    row = piece([warped_ref[p] for p in range(16)], False)
    store = pltpu.make_async_copy(cc_ref, cc_hbm.at[0], local_sem.at[0])
    store.start()
    second_y, second = start_gather(1, row)
    second.wait_recv()
    regular, scale = regular_of(grid_of(rows[1].reshape(128, 128), 32))
    for tile in range(3):
        value = before[tile] + regular[tile] * scale
        velocity_ref[tile, 0] = value[:, 0:64]
        velocity_ref[tile, 1] = value[:, 64:128]
    for copy in halos:
        copy.wait_send()
    for copy in (first_y, first, second_y, second):
        copy.wait_send()
    store.wait()


def per_device(fixed, moving, block_place, tissue):
    vmem = pltpu.VMEM
    return pl.pallas_call(
        kernel,
        out_shape=(
            jax.ShapeDtypeStruct((3, 2, 32, 64), F32),
            jax.ShapeDtypeStruct((1, 8, 32, 128), F32),
        ),
        in_specs=[
            pl.BlockSpec(memory_space=pltpu.HBM),
            pl.BlockSpec(memory_space=pltpu.HBM),
            pl.BlockSpec(memory_space=pltpu.SMEM),
            pl.BlockSpec(memory_space=pltpu.SMEM),
        ],
        out_specs=(
            pl.BlockSpec(memory_space=pltpu.VMEM),
            pl.BlockSpec(memory_space=pl.ANY),
        ),
        scratch_shapes=[
            vmem((8, 32, 128), BF16),
            vmem((8, 32, 128), BF16),
            vmem((2, 4, 32, 128), BF16),
            vmem((2, 5, 32, 128), BF16),
            vmem((16, 32, 128), F32),
            vmem((18, 32, 128), F32),
            vmem((512, 128), F32),
            vmem((512, 128), F32),
            vmem((16, 32, 128), F32),
            vmem((256, 256), BF16),
            vmem((256, 128), BF16),
            vmem((256, 256), BF16),
            vmem((128, 128), BF16),
            vmem((384, 128), BF16),
            vmem((256, 768), BF16),
            vmem((5, 8, 32, 128), F32),
            vmem((5, 256, 256), BF16),
            vmem((3, 256, 128), F32),
            vmem((2, 256, 128), F32),
            vmem((8, 32, 128), F32),
            vmem((512, 384), BF16),
            vmem((256, 256), BF16),
            vmem((2, NY, 1, 128), F32),
            vmem((2, 128, 1, 128), F32),
            pltpu.SemaphoreType.DMA((2,)),
            pltpu.SemaphoreType.DMA((4,)),
            pltpu.SemaphoreType.DMA((4,)),
            pltpu.SemaphoreType.DMA((4,)),
            pltpu.SemaphoreType.DMA((4,)),
            pltpu.SemaphoreType.REGULAR((2,)),
        ],
        compiler_params=pltpu.CompilerParams(
            collective_id=0, has_side_effects=True, vmem_limit_bytes=32 * 1024 * 1024
        ),
    )(
        pltpu.with_memory_space_constraint(fixed, pltpu.HBM),
        pltpu.with_memory_space_constraint(moving, pltpu.HBM),
        block_place,
        tissue,
    )


def solution(mesh):
    return jax.shard_map(
        per_device,
        mesh=mesh,
        in_specs=(P("blk", "gz", None, None), P("blk", "gz", None, None), P("blk"), P("blk")),
        out_specs=(P(), P("blk", "gz", None, None)),
        check_vma=False,
    )
```

```python
import functools
import math

import jax
import jax.numpy as jnp
from jax import lax
from jax.experimental import pallas as pl
from jax.experimental.pallas import tpu as pltpu
from jax.sharding import PartitionSpec as P

NX, NY, NZC = 4, 4, 16
F32, BF16 = jnp.float32, jnp.bfloat16
EPSILON = 1e-05
STEP_LENGTH = 0.5
RAW = [math.exp(-(t * t) / 4.5) for t in range(4)]
TOTAL = RAW[0] + 2 * (RAW[1] + RAW[2] + RAW[3])
W1, W2, W3 = (RAW[t] / TOTAL for t in (1, 2, 3))
WIDE = 10
PLACE_LANE = 60
MESH = pl.DeviceIdType.MESH


def coordinates():
    blk = lax.axis_index("blk")
    return blk // (2 * NZC), lax.axis_index("gz"), (blk // 2) % NZC, blk % 2


def device(x, y, z, core):
    return ((x * NZC + z) * 2 + core, y)


def far_first():
    steps = [(z, x, c) for z in range(NZC) for x in range(NX) for c in range(2)][1:]
    return sorted(steps, key=lambda s: -(min(s[0], NZC - s[0]) + min(s[1], NX - s[1]) + 0.3 * s[2]))


def peers():
    x, y, z, core = coordinates()
    along_y = [device(x, (y + d) % NY, z, core) for d in range(1, NY)]
    along_x = [device((x + d // 2) % NX, y, z, (core + d) % 2) for d in range(1, 2 * NX)]
    along_z = {d: device(x, y, (z + d) % NZC, core) for d in (1, 2, 3, 6, 10, 13, 14, 15)}
    others = [
        device((x + dx) % NX, y, (z + dz) % NZC, (core + dc) % 2) for dz, dx, dc in far_first()
    ]
    return along_y, along_x, along_z, others


def iota(shape, dim):
    return lax.broadcasted_iota(jnp.int32, shape, dim)


def lane_parts(shape):
    lane = iota(shape, len(shape) - 1) & 63
    group = (lane * 205) >> 11
    return group, lane - WIDE * group


def split(value):
    high = value.astype(BF16)
    return high, (value - high.astype(F32)).astype(BF16)


def group_weight(t):
    near = jnp.minimum(t, 15 - t)
    out = jnp.where(near >= 3, 1.0, 0.0)
    for at, value in (
        (2, 1 - W3),
        (1, 1 - W3 - W2),
        (0, 1 - W3 - W2 - W1),
        (-1, W1 + W2 + W3),
        (-2, W2 + W3),
        (-3, W3),
    ):
        out = jnp.where(near == at, value, out)
    return out


def hat_tri(where, mark):
    gap = where - mark
    hat = lambda d: jnp.maximum(0.0, 1.0 - jnp.abs(d))
    return 0.5 * hat(gap) + 0.25 * (hat(gap - 1.0) + hat(gap + 1.0))


def own_sums(a):
    mid = a[3] + a[4]
    out0 = (a[0] + a[1]) + (a[2] + mid)
    out1 = out0 + a[5]
    out2 = out1 + a[6]
    out3 = out2 + a[7]
    out7 = mid + (a[5] + (a[6] + a[7]))
    out6 = out7 + a[2]
    out5 = out6 + a[1]
    return [out0, out1, out2, out3, out3, out5, out6, out7]


def side_sums(low, high):
    out3 = low[3]
    out2 = low[2] + out3
    out1 = low[1] + out2
    out0 = low[0] + out1
    out4 = high[0]
    out5 = out4 + high[1]
    out6 = out5 + high[2]
    out7 = out6 + high[3]
    return [out0, out1, out2, out3, out4, out5, out6, out7]


def shifted(value, amount, dim):
    size = value.shape[dim]
    at = iota(value.shape, dim)
    edge = 0 if amount == 1 else size - 1
    return jnp.where(at == edge, 0.0, pltpu.roll(value, amount % size, dim))


def kernel(
    fixed_hbm, moving_hbm, place_ref, tissue_ref,
    velocity_ref, cc_hbm,
    own_i, own_j, halo_i, halo_j,
    image_i, image_j, slope_x, slope_y, warped_ref,
    box_rows, box_cols, grad_rows, grad_cols, gauss_cols, to_cols,
    inner_sums, sums, means, stat_i, cc_ref, combine, before,
    rows_y, rows, local_sem, halo_send, halo_recv, gather_send, gather_recv, known,
):
    gz = lax.axis_index("gz")
    along_y, along_x, along_z, others = peers()
    near_z = [along_z[d] for d in (1, 2, 3, 13, 14, 15)]
    barrier = pltpu.get_barrier_semaphore()
    for peer in along_y + along_x + near_z:
        pl.semaphore_signal(barrier, inc=1, device_id=peer, device_id_type=MESH)
    load_j = pltpu.make_async_copy(moving_hbm.at[0], own_j, local_sem.at[0])
    load_i = pltpu.make_async_copy(fixed_hbm.at[0], own_i, local_sem.at[1])
    load_j.start()
    load_i.start()
    pl.semaphore_wait(barrier, len(along_y) + len(along_x) + len(near_z))

    up, down = along_y[0], along_y[2]
    halos = []
    for index, (source, target, peer) in enumerate(
        (
            (moving_hbm.at[0, 4:8], halo_j.at[0, 1:5], up),
            (moving_hbm.at[0, 0:4], halo_j.at[1, 0:4], down),
            (fixed_hbm.at[0, 4:8], halo_i.at[0], up),
            (fixed_hbm.at[0, 0:4], halo_i.at[1], down),
            (moving_hbm.at[0, 3:4], halo_j.at[0, 0:1], up),
            (moving_hbm.at[0, 4:5], halo_j.at[1, 4:5], down),
        )
    ):
        copy = pltpu.make_async_remote_copy(
            source, target, halo_send.at[index], halo_recv.at[index],
            device_id=peer, device_id_type=MESH,
        )
        copy.start()
        halos.append(copy)
    for peer in near_z:
        pl.semaphore_signal(known.at[0], inc=1, device_id=peer, device_id_type=MESH)

    r, c = iota((256, 256), 0), iota((256, 256), 1)
    same = (r >> 5) == (c >> 5)
    box_rows[...] = jnp.where(same & (jnp.abs(r - c) <= 4), 1.0, 0.0).astype(BF16)
    grad_rows[...] = jnp.where(
        same & (c - r == 1), 0.5, jnp.where(same & (r - c == 1), -0.5, 0.0)
    ).astype(BF16)
    r, c = iota((128, 128), 0), iota((128, 128), 1)
    band = jnp.where(jnp.abs(r - c) <= 4, 1.0, 0.0).astype(BF16)
    box_cols[0:128, :] = band
    box_cols[128:256, :] = band
    grad_cols[...] = jnp.where(r - c == 1, 0.5, jnp.where(c - r == 1, -0.5, 0.0)).astype(BF16)
    turn = lane_parts((128, 128))[1] - 1
    weight = jnp.zeros((128, 128), F32)
    for step, share in ((-1, 0.25), (0, 0.5), (1, 0.25)):
        b = turn + step
        weight = weight + jnp.where((b >= 0) & (b < 8), share * group_weight(r - 16 * b), 0.0)
    high, low = split(weight)
    gauss_cols[0:128, :] = high
    gauss_cols[128:256, :] = high
    gauss_cols[256:384, :] = low

    inside_low = jnp.where(gz > 0, 1.0, 0.0)
    inside_high = jnp.where(gz < NY - 1, 1.0, 0.0)
    load_j.wait()
    load_i.wait()
    for p in range(8):
        image_i[4 + p] = own_i[p].astype(F32)
        image_j[5 + p] = own_j[p].astype(F32)
    flat = own_j[...].reshape(256, 128)
    slope_x[128:384, :] = jnp.dot(grad_rows[...], flat, preferred_element_type=F32)
    slope_y[128:384, :] = jnp.dot(flat, grad_cols[...], preferred_element_type=F32)

    def box_sums(slot):
        field = jnp.dot(box_rows[...], sums[slot], preferred_element_type=F32)
        high, low = split(field[:, :128] + field[:, 128:])
        field = jnp.dot(
            jnp.concatenate([high, low], axis=1), box_cols[...], preferred_element_type=F32
        )
        return field * (1.0 / 729.0)

    def products(fixed, moved):
        return (
            fixed,
            [a * a for a in fixed],
            moved,
            [b * b for b in moved],
            [a * b for a, b in zip(fixed, moved)],
        )

    def put_sums(slot, chunk, inner, outer):
        for p in range(8):
            high, low = split(inner[p] + outer[p])
            at = pl.ds(32 * p + 16 * chunk, 16)
            sums[slot, at, 0:128] = high
            sums[slot, at, 128:256] = low

    for chunk in range(2):
        at = pl.ds(16 * chunk, 16)
        fixed = [image_i[4 + p, at, :] for p in range(8)]
        moved = [image_j[5 + p, at, :] for p in range(8)]
        for slot, planes in enumerate(products(fixed, moved)):
            for p, value in enumerate(own_sums(planes)):
                inner_sums[slot, p, at, :] = value

    pl.semaphore_wait(known.at[0], len(near_z))
    for d in (6, 10):
        pl.semaphore_signal(known.at[1], inc=1, device_id=along_z[d], device_id_type=MESH)

    for copy in halos[:4]:
        copy.wait_recv()
    for p in range(4):
        image_j[1 + p] = halo_j[0, 1 + p].astype(F32) * inside_low
        image_j[13 + p] = halo_j[1, p].astype(F32) * inside_high
        image_i[p] = halo_i[0, p].astype(F32) * inside_low
        image_i[12 + p] = halo_i[1, p].astype(F32) * inside_high

    depth_weight = []
    for p in range(8):
        at = gz * 8 + p
        first = group_weight(at)
        second = group_weight(at - 16)
        depth_weight.append((0.5 * first + 0.25 * second, 0.25 * first + 0.5 * second))
    lane = iota((32, 128), 1)
    lane_group, lane_turn = lane_parts((32, 128))
    row_weight = group_weight(iota((32, 128), 0) - 16 * (lane >> 6))
    place = place_ref[0]
    tissue = tissue_ref[0].astype(F32)

    def piece(planes, first):
        totals = [None] * 6
        for p in range(8):
            at = pl.ds(32 * p, 32)
            mean_i, var_i = stat_i[0, at, :], stat_i[1, at, :]
            mean_w = means[0, at, :]
            var_w = means[1, at, :] - mean_w * mean_w
            cov = means[2, at, :] - mean_i * mean_w
            denom = var_i * var_w + EPSILON
            ratio = cov / denom
            if not first:
                cc_ref[p] = cov * ratio
            image = image_i[4 + p]
            mid = planes[4 + p]
            dcc = 2.0 * ratio * (image - mean_i - cov / (var_w + EPSILON) * (mid - mean_w))
            if first:
                along_rows = slope_x[128 + 32 * p : 160 + 32 * p, :]
                along_cols = slope_y[128 + 32 * p : 160 + 32 * p, :]
            else:
                along_rows = 0.5 * (shifted(mid, -1, 0) - shifted(mid, 1, 0))
                along_cols = 0.5 * (shifted(mid, -1, 1) - shifted(mid, 1, 1))
            along_depth = 0.5 * (planes[5 + p] - planes[3 + p])
            for c, slope in enumerate((along_depth, along_rows, along_cols)):
                force = dcc * slope
                for k in range(2):
                    term = depth_weight[p][k] * force
                    totals[2 * c + k] = term if p == 0 else totals[2 * c + k] + term
        stack = []
        for ck in range(6):
            high, low = split(totals[ck])
            stack.append(jnp.concatenate([high, low, high], axis=1))
        parts = jnp.dot(
            jnp.concatenate(stack, axis=0), gauss_cols[...], preferred_element_type=F32
        )
        merged = jnp.zeros((32, 128), F32)
        for ck in range(6):
            merged = jnp.where(lane_group == ck, parts[32 * ck : 32 * ck + 32], merged)
        row = jnp.sum(merged * row_weight, axis=0, keepdims=True) * tissue
        lane_row = iota((1, 128), 1)
        return jnp.where(lane_row == PLACE_LANE, place.astype(F32) * 0.25, row)

    def exchange(source, targets, everything, sem, partners):
        for d, peer in enumerate(partners):
            pltpu.make_async_remote_copy(
                source, targets.at[d + 1], gather_send.at[sem], gather_recv.at[sem],
                device_id=peer, device_id_type=MESH,
            ).start()
        return pltpu.make_async_remote_copy(
            everything, everything, gather_send.at[sem], gather_recv.at[sem],
            device_id=partners[0], device_id_type=MESH,
        )

    def start_gather(turn, row):
        mine, every = rows_y.at[turn], rows.at[turn]
        rows_y[turn, 0] = row
        done_y = exchange(mine.at[0], mine, mine.at[1:NY], 2 * turn, along_y)
        if turn == 0:
            pl.semaphore_wait(known.at[1], 2)
        done_y.wait_recv()
        rows[turn, 0] = (rows_y[turn, 0] + rows_y[turn, 2]) + (rows_y[turn, 1] + rows_y[turn, 3])
        return done_y, exchange(every.at[0], every, every.at[1:128], 2 * turn + 1, others)

    for chunk in range(2):
        at = pl.ds(16 * chunk, 16)
        fixed = [image_i[p, at, :] for p in (0, 1, 2, 3, 12, 13, 14, 15)]
        moved = [image_j[1 + p, at, :] for p in (0, 1, 2, 3, 12, 13, 14, 15)]
        for slot, planes in enumerate(products(fixed, moved)):
            inner = [inner_sums[slot, p, at, :] for p in range(8)]
            put_sums(slot, chunk, inner, side_sums(planes[:4], planes[4:]))
    mean_i = box_sums(0)
    stat_i[0] = mean_i
    stat_i[1] = box_sums(1) - mean_i * mean_i
    for slot in range(3):
        means[slot] = box_sums(2 + slot)
    row = piece([image_j[1 + p] for p in range(16)], True)
    first_y, first = start_gather(0, row)

    own_row, own_col = place >> 3, place & 7
    r, c = iota((128, 128), 0), iota((128, 128), 1)
    inner = (own_col * 128 + c).astype(F32)
    inner = jnp.clip((inner + 0.5) * (1.0 / 16.0) - 0.5, 0.0, 63.0)
    turn = (r & 63) - WIDE * (((r & 63) * 205) >> 11) - 1
    for first_row, col in ((0, own_col - jnp.where(r < 64, 1, 0)), (256, own_col + 1)):
        gap = inner - (8 * col + turn).astype(F32)
        weight = jnp.maximum(0.0, 1.0 - jnp.abs(gap)).astype(BF16)
        to_cols[first_row : first_row + 128, :] = weight
        if first_row == 0:
            to_cols[128:256, :] = weight

    for copy in halos[4:]:
        copy.wait_recv()
    image_j[0] = halo_j[0, 0].astype(F32) * inside_low
    image_j[17] = halo_j[1, 4].astype(F32) * inside_high
    for start, side, offset in ((0, 0, 1), (384, 1, 0)):
        flat = halo_j[side, offset : offset + 4].reshape(128, 128)
        slope_x[start : start + 128, :] = jnp.dot(
            grad_rows[0:128, 0:128], flat, preferred_element_type=F32
        )
        slope_y[start : start + 128, :] = jnp.dot(
            flat, grad_cols[...], preferred_element_type=F32
        )

    first.wait_recv()
    gathered = rows[0].reshape(128, 128)

    spot = jnp.broadcast_to(gathered[:, PLACE_LANE : PLACE_LANE + 1], (128, 128))
    r, c = iota((128, 128), 0), iota((128, 128), 1)
    spot = jnp.sum(jnp.where(r == c, spot, 0.0), axis=0, keepdims=True).astype(jnp.int32)
    mark = ((spot >> 3) * 2).astype(F32)
    mark = jnp.broadcast_to(jnp.concatenate([mark, mark + 1.0], axis=1), (32, 256))
    spot_col = jnp.broadcast_to(jnp.concatenate([spot & 7, spot & 7], axis=1), (32, 256))
    at = iota((32, 256), 0)
    filtered = hat_tri(at.astype(F32), mark)
    inner = (own_row * 32 + at).astype(F32)
    inner = hat_tri(jnp.clip((inner + 0.5) * (1.0 / 16.0) - 0.5, 0.0, 31.0), mark)
    for d in range(3):
        value = jnp.where(spot_col == own_col + (d - 1), inner, 0.0)
        combine[32 * d : 32 * d + 32, :] = value.astype(BF16)
    for col in range(8):
        value = jnp.where(spot_col == col, filtered, 0.0)
        combine[96 + 32 * col : 128 + 32 * col, :] = value.astype(BF16)

    first_half = iota((128, 128), 1) < 64
    groups, turns = lane_parts((32, 128))

    def combined(gathered, start):
        turned = pltpu.roll(gathered, 64, 1)
        right = lambda high, low: jnp.where(first_half, high, low - low.astype(BF16).astype(F32))
        both = jnp.concatenate([right(gathered, turned), right(turned, gathered)], axis=0)
        value = jnp.dot(combine[start:352, :], both.astype(BF16), preferred_element_type=F32)
        return value + pltpu.roll(value, 64, 1)

    def regular_of(grid):
        cols = [grid[32 * col : 32 * col + 32] for col in range(8)]
        out = []
        squares = jnp.zeros((32, 128), F32)
        inside = (turns >= 1) & (turns <= 8) & (groups < 6) & (iota((32, 128), 1) < 64)
        for col in range(8):
            value = cols[col]
            if col > 0:
                value = value + jnp.where(turns == 1, pltpu.roll(cols[col - 1], 120, 1), 0.0)
            if col < 7:
                value = value + jnp.where(turns == 8, pltpu.roll(cols[col + 1], 8, 1), 0.0)
            value = jnp.where(inside, value, 0.0)
            squares = squares + value * value
            out.append(value)
        mean = jnp.sum(squares, keepdims=True) * (1.0 / (6 * 32 * 64))
        return out, STEP_LENGTH / jnp.sqrt(mean + EPSILON)

    grid = combined(gathered, 0)
    half = first_half[0:32]
    near = jnp.where(half, grid[0:32], grid[32:64])
    high, low = split(near)
    above_high, above_low = split(grid[64:96])
    above = jnp.where(half, above_high.astype(F32), above_low.astype(F32)).astype(BF16)
    wide = jnp.concatenate([high, low, above], axis=1)
    group_wide = jnp.concatenate([groups, groups, groups], axis=1)
    stack = [jnp.where(group_wide == ck, wide, jnp.zeros_like(wide)) for ck in range(6)]
    moves = jnp.dot(jnp.concatenate(stack, axis=0), to_cols[...], preferred_element_type=F32)
    regular, scale = regular_of(grid[96:352])
    for col in range(8):
        before[col] = regular[col] * scale
    moves = moves * scale
    shift = []
    for c in range(3):
        value, other = moves[64 * c : 64 * c + 32], moves[64 * c + 32 : 64 * c + 64]
        shift.append((value, other - value))

    for p in range(16):
        deep = (gz * 8 + (p - 4)).astype(F32)
        part = jnp.clip((deep + 0.5) * (1.0 / 16.0) - 0.5, 0.0, 1.0)
        value = image_j[1 + p]
        slopes = (
            0.5 * (image_j[2 + p] - image_j[p]),
            slope_x[32 * p : 32 * p + 32, :],
            slope_y[32 * p : 32 * p + 32, :],
        )
        for (base, rise), slope in zip(shift, slopes):
            value = value + (base + part * rise) * slope
        if p < 4:
            value = value * inside_low
        if p >= 12:
            value = value * inside_high
        warped_ref[p] = value
    for chunk in range(2):
        at = pl.ds(16 * chunk, 16)
        fixed = [image_i[p, at, :] for p in range(16)]
        moved = [warped_ref[p, at, :] for p in range(16)]
        for slot, planes in enumerate(products(fixed, moved)):
            if slot >= 2:
                put_sums(
                    slot, chunk, own_sums(planes[4:12]), side_sums(planes[0:4], planes[12:16])
                )
    for slot in range(3):
        means[slot] = box_sums(2 + slot)
    row = piece([warped_ref[p] for p in range(16)], False)
    store = pltpu.make_async_copy(cc_ref, cc_hbm.at[0], local_sem.at[0])
    store.start()
    second_y, second = start_gather(1, row)
    second.wait_recv()
    regular, scale = regular_of(combined(rows[1].reshape(128, 128), 96))
    total = [before[col] + regular[col] * scale for col in range(8)]
    lane_col = iota((32, 128), 1) >> 3
    for ck in range(6):
        value = jnp.zeros((32, 128), F32)
        for col in range(8):
            moved = pltpu.roll(total[col], (8 * col - WIDE * ck - 1) % 128, 1)
            value = jnp.where(lane_col == col, moved, value)
        velocity_ref[ck // 2, ck % 2] = value[:, 0:64]
    for copy in halos:
        copy.wait_send()
    for copy in (first_y, first, second_y, second):
        copy.wait_send()
    store.wait()


def per_device(fixed, moving, block_place, tissue):
    vmem = pltpu.VMEM
    return pl.pallas_call(
        kernel,
        out_shape=(
            jax.ShapeDtypeStruct((3, 2, 32, 64), F32),
            jax.ShapeDtypeStruct((1, 8, 32, 128), F32),
        ),
        in_specs=[
            pl.BlockSpec(memory_space=pltpu.HBM),
            pl.BlockSpec(memory_space=pltpu.HBM),
            pl.BlockSpec(memory_space=pltpu.SMEM),
            pl.BlockSpec(memory_space=pltpu.SMEM),
        ],
        out_specs=(
            pl.BlockSpec(memory_space=pltpu.VMEM),
            pl.BlockSpec(memory_space=pl.ANY),
        ),
        scratch_shapes=[
            vmem((8, 32, 128), BF16),
            vmem((8, 32, 128), BF16),
            vmem((2, 4, 32, 128), BF16),
            vmem((2, 5, 32, 128), BF16),
            vmem((16, 32, 128), F32),
            vmem((18, 32, 128), F32),
            vmem((512, 128), F32),
            vmem((512, 128), F32),
            vmem((16, 32, 128), F32),
            vmem((256, 256), BF16),
            vmem((256, 128), BF16),
            vmem((256, 256), BF16),
            vmem((128, 128), BF16),
            vmem((384, 128), BF16),
            vmem((384, 128), BF16),
            vmem((5, 8, 32, 128), F32),
            vmem((5, 256, 256), BF16),
            vmem((3, 256, 128), F32),
            vmem((2, 256, 128), F32),
            vmem((8, 32, 128), F32),
            vmem((352, 256), BF16),
            vmem((8, 32, 128), F32),
            vmem((2, NY, 1, 128), F32),
            vmem((2, 128, 1, 128), F32),
            pltpu.SemaphoreType.DMA((2,)),
            pltpu.SemaphoreType.DMA((6,)),
            pltpu.SemaphoreType.DMA((6,)),
            pltpu.SemaphoreType.DMA((4,)),
            pltpu.SemaphoreType.DMA((4,)),
            pltpu.SemaphoreType.REGULAR((2,)),
        ],
        compiler_params=pltpu.CompilerParams(
            collective_id=0, has_side_effects=True, vmem_limit_bytes=32 * 1024 * 1024
        ),
    )(
        pltpu.with_memory_space_constraint(fixed, pltpu.HBM),
        pltpu.with_memory_space_constraint(moving, pltpu.HBM),
        block_place,
        tissue,
    )


def solution(mesh):
    return jax.shard_map(
        per_device,
        mesh=mesh,
        in_specs=(P("blk", "gz", None, None), P("blk", "gz", None, None), P("blk"), P("blk")),
        out_specs=(P(), P("blk", "gz", None, None)),
        check_vma=False,
    )
```

```python
import functools
import math

import jax
import jax.numpy as jnp
from jax import lax
from jax.experimental import pallas as pl
from jax.experimental.pallas import tpu as pltpu
from jax.sharding import PartitionSpec as P

NX, NY, NZC = 4, 4, 16
F32, BF16 = jnp.float32, jnp.bfloat16
EPSILON = 1e-05
STEP_LENGTH = 0.5
RAW = [math.exp(-(t * t) / 4.5) for t in range(4)]
TOTAL = RAW[0] + 2 * (RAW[1] + RAW[2] + RAW[3])
W1, W2, W3 = (RAW[t] / TOTAL for t in (1, 2, 3))
WIDE = 10
PLACE_LANE = 60
MESH = pl.DeviceIdType.MESH
ROUNDS = (1, 2, 4, 1)


def coordinates():
    blk = lax.axis_index("blk")
    return blk // (2 * NZC), lax.axis_index("gz"), (blk // 2) % NZC, blk % 2


def far_first():
    steps = [(z, x, c) for z in range(NZC) for x in range(NX) for c in range(2)][1:]
    return sorted(steps, key=lambda s: -(4 * min(s[0], NZC - s[0]) + min(s[1], NX - s[1]) + 0.3 * s[2]))


def peers():
    x, y, z, core = coordinates()
    at_x = [(x + d) % NX * (2 * NZC) for d in range(NX)]
    at_z = [(z + d) % NZC * 2 for d in range(NZC)]
    at_core = [core, 1 - core]
    base = x * (2 * NZC) + z * 2 + core
    along_y = [(base, (y + d) % NY) for d in (2, 1, 3)]
    along_x = [(at_x[d // 2] + at_z[0] + at_core[d % 2], y) for d in range(1, 2 * NX)]
    along_z = {d: (at_x[0] + at_z[d % NZC] + core, y) for d in (1, 2, 4, -1, -2, -4)}
    others = [(at_x[dx] + at_z[dz] + at_core[dc], y) for dz, dx, dc in far_first()]
    return along_y, along_x, along_z, others


def iota(shape, dim):
    return lax.broadcasted_iota(jnp.int32, shape, dim)


def lane_parts(shape):
    lane = iota(shape, len(shape) - 1) & 63
    group = (lane * 205) >> 11
    return group, lane - WIDE * group


def split(value):
    high = value.astype(BF16)
    return high, (value - high.astype(F32)).astype(BF16)


def group_weight(t):
    near = jnp.minimum(t, 15 - t)
    out = jnp.where(near >= 3, 1.0, 0.0)
    for at, value in (
        (2, 1 - W3),
        (1, 1 - W3 - W2),
        (0, 1 - W3 - W2 - W1),
        (-1, W1 + W2 + W3),
        (-2, W2 + W3),
        (-3, W3),
    ):
        out = jnp.where(near == at, value, out)
    return out


def hat_tri(where, mark):
    gap = where - mark
    hat = lambda d: jnp.maximum(0.0, 1.0 - jnp.abs(d))
    return 0.5 * hat(gap) + 0.25 * (hat(gap - 1.0) + hat(gap + 1.0))


def own_sums(a):
    mid = a[3] + a[4]
    out0 = (a[0] + a[1]) + (a[2] + mid)
    out1 = out0 + a[5]
    out2 = out1 + a[6]
    out3 = out2 + a[7]
    out7 = mid + (a[5] + (a[6] + a[7]))
    out6 = out7 + a[2]
    out5 = out6 + a[1]
    return [out0, out1, out2, out3, out3, out5, out6, out7]


def side_sums(low, high):
    out3 = low[3]
    out2 = low[2] + out3
    out1 = low[1] + out2
    out0 = low[0] + out1
    out4 = high[0]
    out5 = out4 + high[1]
    out6 = out5 + high[2]
    out7 = out6 + high[3]
    return [out0, out1, out2, out3, out4, out5, out6, out7]


def shifted(value, amount, dim):
    size = value.shape[dim]
    at = iota(value.shape, dim)
    edge = 0 if amount == 1 else size - 1
    return jnp.where(at == edge, 0.0, pltpu.roll(value, amount % size, dim))


def kernel(
    fixed_hbm, moving_hbm, place_in, tissue_in,
    velocity_ref, cc_ref,
    own_i, own_j, halo_i, halo_j,
    image_i, image_j, slope_x, slope_y, warped_ref,
    box_rows, box_cols, grad_rows, grad_cols, gauss_cols, to_cols,
    inner_sums, sums, means, stat_i, combine, before,
    rows_y, rows, place_ref, tissue_ref, local_sem, halo_send, halo_recv, gather_send, gather_recv, known,
):
    gz = lax.axis_index("gz")
    along_y, along_x, along_z, others = peers()
    next_z = [along_z[1], along_z[-1]]
    barrier = pltpu.get_barrier_semaphore()
    for peer in along_y + along_x + next_z:
        pl.semaphore_signal(barrier, inc=1, device_id=peer, device_id_type=MESH)
    load_j = pltpu.make_async_copy(moving_hbm.at[0], own_j, local_sem.at[0])
    load_i = pltpu.make_async_copy(fixed_hbm.at[0], own_i, local_sem.at[1])
    load_place = pltpu.make_async_copy(place_in, place_ref, local_sem.at[2])
    load_tissue = pltpu.make_async_copy(tissue_in, tissue_ref, local_sem.at[3])
    load_j.start()
    load_i.start()
    load_place.start()
    load_tissue.start()
    pl.semaphore_wait(barrier, len(along_y) + len(along_x) + len(next_z))

    up, down = along_y[1], along_y[2]
    halos = []
    for index, (source, target, peer) in enumerate(
        (
            (fixed_hbm.at[0, 4:8], halo_i.at[0], up),
            (fixed_hbm.at[0, 0:4], halo_i.at[1], down),
            (moving_hbm.at[0, 4:8], halo_j.at[0, 1:5], up),
            (moving_hbm.at[0, 0:4], halo_j.at[1, 0:4], down),
            (moving_hbm.at[0, 3:4], halo_j.at[0, 0:1], up),
            (moving_hbm.at[0, 4:5], halo_j.at[1, 4:5], down),
        )
    ):
        copy = pltpu.make_async_remote_copy(
            source, target, halo_send.at[index], halo_recv.at[index],
            device_id=peer, device_id_type=MESH,
        )
        copy.start()
        halos.append(copy)
    def tell(index):
        for d in (ROUNDS[index], -ROUNDS[index]):
            pl.semaphore_signal(known.at[index], inc=1, device_id=along_z[d], device_id_type=MESH)

    tell(0)

    r, c = iota((256, 256), 0), iota((256, 256), 1)
    same = (r >> 5) == (c >> 5)
    box_rows[...] = jnp.where(same & (jnp.abs(r - c) <= 4), 1.0, 0.0).astype(BF16)
    grad_rows[...] = jnp.where(
        same & (c - r == 1), 0.5, jnp.where(same & (r - c == 1), -0.5, 0.0)
    ).astype(BF16)
    r, c = iota((128, 128), 0), iota((128, 128), 1)
    band = jnp.where(jnp.abs(r - c) <= 4, 1.0, 0.0).astype(BF16)
    box_cols[0:128, :] = band
    box_cols[128:256, :] = band
    grad_cols[...] = jnp.where(r - c == 1, 0.5, jnp.where(c - r == 1, -0.5, 0.0)).astype(BF16)
    turn = lane_parts((128, 128))[1] - 1
    weight = jnp.zeros((128, 128), F32)
    for step, share in ((-1, 0.25), (0, 0.5), (1, 0.25)):
        b = turn + step
        weight = weight + jnp.where((b >= 0) & (b < 8), share * group_weight(r - 16 * b), 0.0)
    high, low = split(weight)
    gauss_cols[0:128, :] = high
    gauss_cols[128:256, :] = high
    gauss_cols[256:384, :] = low

    inside_low = jnp.where(gz > 0, 1.0, 0.0)
    inside_high = jnp.where(gz < NY - 1, 1.0, 0.0)
    load_j.wait()
    load_i.wait()
    load_place.wait()
    load_tissue.wait()
    for p in range(8):
        image_i[4 + p] = own_i[p].astype(F32)
        image_j[5 + p] = own_j[p].astype(F32)
    flat = own_j[...].reshape(256, 128)
    slope_x[128:384, :] = jnp.dot(grad_rows[...], flat, preferred_element_type=F32)
    slope_y[128:384, :] = jnp.dot(flat, grad_cols[...], preferred_element_type=F32)

    def box_sums(slot):
        field = jnp.dot(box_rows[...], sums[slot], preferred_element_type=F32)
        high, low = split(field[:, :128] + field[:, 128:])
        field = jnp.dot(
            jnp.concatenate([high, low], axis=1), box_cols[...], preferred_element_type=F32
        )
        return field * (1.0 / 729.0)

    def products(fixed, moved):
        return (
            fixed,
            [a * a for a in fixed],
            moved,
            [b * b for b in moved],
            [a * b for a, b in zip(fixed, moved)],
        )

    def put_sums(slot, chunk, inner, outer):
        for p in range(8):
            high, low = split(inner[p] + outer[p])
            at = pl.ds(32 * p + 16 * chunk, 16)
            sums[slot, at, 0:128] = high
            sums[slot, at, 128:256] = low

    for chunk in range(2):
        at = pl.ds(16 * chunk, 16)
        fixed = [image_i[4 + p, at, :] for p in range(8)]
        moved = [image_j[5 + p, at, :] for p in range(8)]
        for slot, planes in enumerate(products(fixed, moved)):
            for p, value in enumerate(own_sums(planes)):
                inner_sums[slot, p, at, :] = value

    pl.semaphore_wait(known.at[0], 2)
    tell(1)
    pl.semaphore_wait(known.at[1], 2)
    tell(2)

    for copy in halos[:2]:
        copy.wait_recv()
    for p in range(4):
        image_i[p] = halo_i[0, p].astype(F32) * inside_low
        image_i[12 + p] = halo_i[1, p].astype(F32) * inside_high

    depth_weight = []
    for p in range(8):
        at = gz * 8 + p
        first = group_weight(at)
        second = group_weight(at - 16)
        depth_weight.append((0.5 * first + 0.25 * second, 0.25 * first + 0.5 * second))
    lane = iota((32, 128), 1)
    lane_group, lane_turn = lane_parts((32, 128))
    row_weight = group_weight(iota((32, 128), 0) - 16 * (lane >> 6))
    place = place_ref[0]
    tissue = tissue_ref[0].astype(F32)

    def piece(images, first):
        totals = [None] * 6
        for p in range(8):
            at = pl.ds(32 * p, 32)
            mean_i, var_i = stat_i[0, at, :], stat_i[1, at, :]
            mean_w = means[0, at, :]
            var_w = means[1, at, :] - mean_w * mean_w
            cov = means[2, at, :] - mean_i * mean_w
            denom = var_i * var_w + EPSILON
            ratio = cov / denom
            if not first:
                cc_ref[0, p] = cov * ratio
            image = image_i[4 + p]
            mid = images[4 + p]
            dcc = 2.0 * ratio * (image - mean_i - cov / (var_w + EPSILON) * (mid - mean_w))
            if first:
                along_rows = slope_x[128 + 32 * p : 160 + 32 * p, :]
                along_cols = slope_y[128 + 32 * p : 160 + 32 * p, :]
            else:
                along_rows = 0.5 * (shifted(mid, -1, 0) - shifted(mid, 1, 0))
                along_cols = 0.5 * (shifted(mid, -1, 1) - shifted(mid, 1, 1))
            along_depth = 0.5 * (images[5 + p] - images[3 + p])
            for c, slope in enumerate((along_depth, along_rows, along_cols)):
                force = dcc * slope
                for k in range(2):
                    term = depth_weight[p][k] * force
                    totals[2 * c + k] = term if p == 0 else totals[2 * c + k] + term
        stack = []
        for ck in range(6):
            high, low = split(totals[ck])
            stack.append(jnp.concatenate([high, low, high], axis=1))
        parts = jnp.dot(
            jnp.concatenate(stack, axis=0), gauss_cols[...], preferred_element_type=F32
        )
        merged = jnp.zeros((32, 128), F32)
        for ck in range(6):
            merged = jnp.where(lane_group == ck, parts[32 * ck : 32 * ck + 32], merged)
        row = jnp.sum(merged * row_weight, axis=0, keepdims=True) * tissue
        lane_row = iota((1, 128), 1)
        return jnp.where(lane_row == PLACE_LANE, place.astype(F32) * 0.25, row)

    unsent = []

    def exchange(source, targets, sem, partners):
        for index, peer in enumerate(partners):
            pltpu.make_async_remote_copy(
                source, targets.at[index], gather_send.at[sem], gather_recv.at[sem],
                device_id=peer, device_id_type=MESH,
            ).start()
        done = pltpu.make_async_remote_copy(
            targets, targets, gather_send.at[sem], gather_recv.at[sem],
            device_id=partners[0], device_id_type=MESH,
        )
        unsent.append(done)
        return done

    def start_gather(turn, row):
        rows_y[turn, 0] = row
        summed = exchange(rows_y.at[turn, 0], rows_y.at[turn, 1:NY], 2 * turn, along_y)
        if turn == 0:
            pl.semaphore_wait(known.at[2], 2)
            tell(3)
        summed.wait_recv()
        every = rows.at[turn]
        rows[turn, 0] = (rows_y[turn, 0] + rows_y[turn, 1]) + (rows_y[turn, 2] + rows_y[turn, 3])
        if turn == 0:
            pl.semaphore_wait(known.at[3], 2)
        return exchange(every.at[0], every.at[1:128], 2 * turn + 1, others)

    def finish_gather(turn, done):
        done.wait_recv()
        return rows[turn].reshape(128, 128)

    def first_sums(slots):
        for chunk in range(2):
            at = pl.ds(16 * chunk, 16)
            fixed = [image_i[p, at, :] for p in (0, 1, 2, 3, 12, 13, 14, 15)]
            moved = [image_j[1 + p, at, :] for p in (0, 1, 2, 3, 12, 13, 14, 15)]
            for slot, planes in enumerate(products(fixed, moved)):
                if slot in slots:
                    inner = [inner_sums[slot, p, at, :] for p in range(8)]
                    put_sums(slot, chunk, inner, side_sums(planes[:4], planes[4:]))

    first_sums((0, 1))
    mean_i = box_sums(0)
    stat_i[0] = mean_i
    stat_i[1] = box_sums(1) - mean_i * mean_i
    for copy in halos[2:4]:
        copy.wait_recv()
    for p in range(4):
        image_j[1 + p] = halo_j[0, 1 + p].astype(F32) * inside_low
        image_j[13 + p] = halo_j[1, p].astype(F32) * inside_high
    first_sums((2, 3, 4))
    for slot in range(3):
        means[slot] = box_sums(2 + slot)
    row = piece([image_j[1 + p] for p in range(16)], True)
    waits = start_gather(0, row)

    own_row, own_col = place >> 3, place & 7
    r, c = iota((128, 128), 0), iota((128, 128), 1)
    inner = (own_col * 128 + c).astype(F32)
    inner = jnp.clip((inner + 0.5) * (1.0 / 16.0) - 0.5, 0.0, 63.0)
    turn = (r & 63) - WIDE * (((r & 63) * 205) >> 11) - 1
    for first_row, col in ((0, own_col - jnp.where(r < 64, 1, 0)), (256, own_col + 1)):
        gap = inner - (8 * col + turn).astype(F32)
        weight = jnp.maximum(0.0, 1.0 - jnp.abs(gap)).astype(BF16)
        to_cols[first_row : first_row + 128, :] = weight
        if first_row == 0:
            to_cols[128:256, :] = weight

    for copy in halos[4:]:
        copy.wait_recv()
    image_j[0] = halo_j[0, 0].astype(F32) * inside_low
    image_j[17] = halo_j[1, 4].astype(F32) * inside_high
    for start, side, offset in ((0, 0, 1), (384, 1, 0)):
        flat = halo_j[side, offset : offset + 4].reshape(128, 128)
        slope_x[start : start + 128, :] = jnp.dot(
            grad_rows[0:128, 0:128], flat, preferred_element_type=F32
        )
        slope_y[start : start + 128, :] = jnp.dot(
            flat, grad_cols[...], preferred_element_type=F32
        )

    gathered = finish_gather(0, waits)

    spot = jnp.broadcast_to(gathered[:, PLACE_LANE : PLACE_LANE + 1], (128, 128))
    r, c = iota((128, 128), 0), iota((128, 128), 1)
    spot = jnp.sum(jnp.where(r == c, spot, 0.0), axis=0, keepdims=True).astype(jnp.int32)
    mark = ((spot >> 3) * 2).astype(F32)
    mark = jnp.broadcast_to(jnp.concatenate([mark, mark + 1.0], axis=1), (32, 256))
    spot_col = jnp.broadcast_to(jnp.concatenate([spot & 7, spot & 7], axis=1), (32, 256))
    at = iota((32, 256), 0)
    filtered = hat_tri(at.astype(F32), mark)
    inner = (own_row * 32 + at).astype(F32)
    inner = hat_tri(jnp.clip((inner + 0.5) * (1.0 / 16.0) - 0.5, 0.0, 31.0), mark)
    for d in range(3):
        value = jnp.where(spot_col == own_col + (d - 1), inner, 0.0)
        combine[32 * d : 32 * d + 32, :] = value.astype(BF16)
    for col in range(8):
        value = jnp.where(spot_col == col, filtered, 0.0)
        combine[96 + 32 * col : 128 + 32 * col, :] = value.astype(BF16)

    first_half = iota((128, 128), 1) < 64
    groups, turns = lane_parts((32, 128))

    def combined(gathered, start):
        turned = pltpu.roll(gathered, 64, 1)
        right = lambda high, low: jnp.where(first_half, high, low - low.astype(BF16).astype(F32))
        both = jnp.concatenate([right(gathered, turned), right(turned, gathered)], axis=0)
        return jnp.dot(combine[start:352, :], both.astype(BF16), preferred_element_type=F32)

    def regular_of(grid):
        low_lanes = first_half[0:16]
        cols = []
        for col in range(8):
            top, bottom = grid[32 * col : 32 * col + 16], grid[32 * col + 16 : 32 * col + 32]
            cols.append(
                jnp.where(low_lanes, top, bottom)
                + pltpu.roll(jnp.where(low_lanes, bottom, top), 64, 1)
            )
        out = []
        squares = jnp.zeros((16, 128), F32)
        group, turn = groups[0:16], turns[0:16]
        inside = (turn >= 1) & (turn <= 8) & (group < 6)
        for col in range(8):
            value = cols[col]
            if col > 0:
                value = value + jnp.where(turn == 1, pltpu.roll(cols[col - 1], 120, 1), 0.0)
            if col < 7:
                value = value + jnp.where(turn == 8, pltpu.roll(cols[col + 1], 8, 1), 0.0)
            value = jnp.where(inside, value, 0.0)
            squares = squares + value * value
            out.append(value)
        mean = jnp.sum(squares, keepdims=True) * (1.0 / (6 * 32 * 64))
        return out, STEP_LENGTH / jnp.sqrt(mean + EPSILON)

    grid = combined(gathered, 0)
    around = grid[0:96] + pltpu.roll(grid[0:96], 64, 1)
    half = first_half[0:32]
    near = jnp.where(half, around[0:32], around[32:64])
    high, low = split(near)
    above_high, above_low = split(around[64:96])
    above = jnp.where(half, above_high.astype(F32), above_low.astype(F32)).astype(BF16)
    wide = jnp.concatenate([high, low, above], axis=1)
    group_wide = jnp.concatenate([groups, groups, groups], axis=1)
    stack = [jnp.where(group_wide == ck, wide, jnp.zeros_like(wide)) for ck in range(6)]
    moves = jnp.dot(jnp.concatenate(stack, axis=0), to_cols[...], preferred_element_type=F32)
    regular, scale = regular_of(grid[96:352])
    for col in range(8):
        before[col] = regular[col] * scale
    moves = moves * scale
    shift = []
    for c in range(3):
        value, other = moves[64 * c : 64 * c + 32], moves[64 * c + 32 : 64 * c + 64]
        shift.append((value, other - value))

    for p in range(16):
        deep = (gz * 8 + (p - 4)).astype(F32)
        part = jnp.clip((deep + 0.5) * (1.0 / 16.0) - 0.5, 0.0, 1.0)
        value = image_j[1 + p]
        slopes = (
            0.5 * (image_j[2 + p] - image_j[p]),
            slope_x[32 * p : 32 * p + 32, :],
            slope_y[32 * p : 32 * p + 32, :],
        )
        for (base, rise), slope in zip(shift, slopes):
            value = value + (base + part * rise) * slope
        if p < 4:
            value = value * inside_low
        if p >= 12:
            value = value * inside_high
        warped_ref[p] = value
    for chunk in range(2):
        at = pl.ds(16 * chunk, 16)
        fixed = [image_i[p, at, :] for p in range(16)]
        moved = [warped_ref[p, at, :] for p in range(16)]
        for slot, planes in enumerate(products(fixed, moved)):
            if slot >= 2:
                put_sums(
                    slot, chunk, own_sums(planes[4:12]), side_sums(planes[0:4], planes[12:16])
                )
    for slot in range(3):
        means[slot] = box_sums(2 + slot)
    row = piece([warped_ref[p] for p in range(16)], False)
    waits = start_gather(1, row)
    regular, scale = regular_of(combined(finish_gather(1, waits), 96))
    total = [before[col] + regular[col] * scale for col in range(8)]
    lane_col = (iota((16, 128), 1) >> 3) & 7
    for ck in range(6):
        value = jnp.zeros((16, 128), F32)
        for col in range(8):
            moved = pltpu.roll(total[col], (8 * col - WIDE * ck - 1) % 128, 1)
            value = jnp.where(lane_col == col, moved, value)
        velocity_ref[ck // 2, ck % 2, 0:16, :] = value[:, 0:64]
        velocity_ref[ck // 2, ck % 2, 16:32, :] = value[:, 64:128]
    for copy in halos:
        copy.wait_send()
    for copy in unsent:
        copy.wait_send()


def per_device(fixed, moving, block_place, tissue):
    vmem = pltpu.VMEM
    return pl.pallas_call(
        kernel,
        out_shape=(
            jax.ShapeDtypeStruct((3, 2, 32, 64), F32),
            jax.ShapeDtypeStruct((1, 8, 32, 128), F32),
        ),
        in_specs=[
            pl.BlockSpec(memory_space=pltpu.HBM),
            pl.BlockSpec(memory_space=pltpu.HBM),
            pl.BlockSpec(memory_space=pltpu.HBM),
            pl.BlockSpec(memory_space=pltpu.HBM),
        ],
        out_specs=(
            pl.BlockSpec(memory_space=pltpu.VMEM),
            pl.BlockSpec(memory_space=pltpu.VMEM),
        ),
        scratch_shapes=[
            vmem((8, 32, 128), BF16),
            vmem((8, 32, 128), BF16),
            vmem((2, 4, 32, 128), BF16),
            vmem((2, 5, 32, 128), BF16),
            vmem((16, 32, 128), F32),
            vmem((18, 32, 128), F32),
            vmem((512, 128), F32),
            vmem((512, 128), F32),
            vmem((16, 32, 128), F32),
            vmem((256, 256), BF16),
            vmem((256, 128), BF16),
            vmem((256, 256), BF16),
            vmem((128, 128), BF16),
            vmem((384, 128), BF16),
            vmem((384, 128), BF16),
            vmem((5, 8, 32, 128), F32),
            vmem((5, 256, 256), BF16),
            vmem((3, 256, 128), F32),
            vmem((2, 256, 128), F32),
            vmem((352, 256), BF16),
            vmem((8, 16, 128), F32),
            vmem((2, NY, 1, 128), F32),
            vmem((2, 128, 1, 128), F32),
            pltpu.SMEM((1,), jnp.int32),
            pltpu.SMEM((1,), jnp.int32),
            pltpu.SemaphoreType.DMA((4,)),
            pltpu.SemaphoreType.DMA((6,)),
            pltpu.SemaphoreType.DMA((6,)),
            pltpu.SemaphoreType.DMA((4,)),
            pltpu.SemaphoreType.DMA((4,)),
            pltpu.SemaphoreType.REGULAR((len(ROUNDS),)),
        ],
        compiler_params=pltpu.CompilerParams(
            collective_id=0, has_side_effects=True, vmem_limit_bytes=32 * 1024 * 1024
        ),
    )(
        pltpu.with_memory_space_constraint(fixed, pltpu.HBM),
        pltpu.with_memory_space_constraint(moving, pltpu.HBM),
        block_place,
        tissue,
    )


def solution(mesh):
    return jax.shard_map(
        per_device,
        mesh=mesh,
        in_specs=(P("blk", "gz", None, None), P("blk", "gz", None, None), P("blk"), P("blk")),
        out_specs=(P(), P("blk", "gz", None, None)),
        check_vma=False,
    )
```

```python
import functools
import math

import jax
import jax.numpy as jnp
from jax import lax
from jax.experimental import pallas as pl
from jax.experimental.pallas import tpu as pltpu
from jax.sharding import PartitionSpec as P

NX, NY, NZC = 4, 4, 16
F32, BF16 = jnp.float32, jnp.bfloat16
EPSILON = 1e-05
STEP_LENGTH = 0.5
RAW = [math.exp(-(t * t) / 4.5) for t in range(4)]
TOTAL = RAW[0] + 2 * (RAW[1] + RAW[2] + RAW[3])
W1, W2, W3 = (RAW[t] / TOTAL for t in (1, 2, 3))
WIDE = 10
PLACE_LANE = 60
MESH = pl.DeviceIdType.MESH
OPPOSITE = 2 * NX
ROUNDS = (1, 2, 4, 1)


def coordinates():
    blk = lax.axis_index("blk")
    return blk // (2 * NZC), lax.axis_index("gz"), (blk // 2) % NZC, blk % 2


def far_first():
    steps = [(z, x, c) for z in range(NZC) for x in range(NX) for c in range(2)][1:]
    return sorted(steps, key=lambda s: -(4 * min(s[0], NZC - s[0]) + min(s[1], NX - s[1]) + 0.3 * s[2]))


def peers():
    x, y, z, core = coordinates()
    at_x = [(x + d) % NX * (2 * NZC) for d in range(NX)]
    at_z = [(z + d) % NZC * 2 for d in range(NZC)]
    at_core = [core, 1 - core]
    base = x * (2 * NZC) + z * 2 + core
    along_y = [(base, (y + d) % NY) for d in (2, 1, 3)]
    along_x = [(at_x[d // 2] + at_z[0] + at_core[d % 2], y) for d in range(1, 2 * NX)]
    along_z = {d: (at_x[0] + at_z[d % NZC] + core, y) for d in (1, 2, 4, -1, -2, -4)}
    others = [(at_x[dx] + at_z[dz] + at_core[dc], y) for dz, dx, dc in far_first()]
    opposite = [(peer, (y + d) % NY) for peer, _ in others[:OPPOSITE] for d in range(NY)]
    return along_y, along_x, along_z, others, opposite


def iota(shape, dim):
    return lax.broadcasted_iota(jnp.int32, shape, dim)


def lane_parts(shape):
    lane = iota(shape, len(shape) - 1) & 63
    group = (lane * 205) >> 11
    return group, lane - WIDE * group


def split(value):
    high = value.astype(BF16)
    return high, (value - high.astype(F32)).astype(BF16)


def group_weight(t):
    near = jnp.minimum(t, 15 - t)
    out = jnp.where(near >= 3, 1.0, 0.0)
    for at, value in (
        (2, 1 - W3),
        (1, 1 - W3 - W2),
        (0, 1 - W3 - W2 - W1),
        (-1, W1 + W2 + W3),
        (-2, W2 + W3),
        (-3, W3),
    ):
        out = jnp.where(near == at, value, out)
    return out


def hat_tri(where, mark):
    gap = where - mark
    hat = lambda d: jnp.maximum(0.0, 1.0 - jnp.abs(d))
    return 0.5 * hat(gap) + 0.25 * (hat(gap - 1.0) + hat(gap + 1.0))


def own_sums(a):
    mid = a[3] + a[4]
    out0 = (a[0] + a[1]) + (a[2] + mid)
    out1 = out0 + a[5]
    out2 = out1 + a[6]
    out3 = out2 + a[7]
    out7 = mid + (a[5] + (a[6] + a[7]))
    out6 = out7 + a[2]
    out5 = out6 + a[1]
    return [out0, out1, out2, out3, out3, out5, out6, out7]


def side_sums(low, high):
    out3 = low[3]
    out2 = low[2] + out3
    out1 = low[1] + out2
    out0 = low[0] + out1
    out4 = high[0]
    out5 = out4 + high[1]
    out6 = out5 + high[2]
    out7 = out6 + high[3]
    return [out0, out1, out2, out3, out4, out5, out6, out7]


def shifted(value, amount, dim):
    size = value.shape[dim]
    at = iota(value.shape, dim)
    edge = 0 if amount == 1 else size - 1
    return jnp.where(at == edge, 0.0, pltpu.roll(value, amount % size, dim))


def kernel(
    fixed_hbm, moving_hbm, place_in, tissue_in,
    velocity_ref, cc_ref,
    own_i, own_j, halo_i, halo_j,
    image_i, image_j, slope_x, slope_y, warped_ref,
    box_rows, box_cols, grad_rows, grad_cols, gauss_cols, to_cols,
    inner_sums, sums, means, stat_i, combine, before,
    rows_y, rows, unsummed, place_ref, tissue_ref, local_sem, halo_send, halo_recv, gather_send, gather_recv, known,
):
    gz = lax.axis_index("gz")
    along_y, along_x, along_z, others, opposite = peers()
    next_z = [along_z[1], along_z[-1]]
    barrier = pltpu.get_barrier_semaphore()
    for peer in along_y + along_x + next_z:
        pl.semaphore_signal(barrier, inc=1, device_id=peer, device_id_type=MESH)
    load_j = pltpu.make_async_copy(moving_hbm.at[0], own_j, local_sem.at[0])
    load_i = pltpu.make_async_copy(fixed_hbm.at[0], own_i, local_sem.at[1])
    load_place = pltpu.make_async_copy(place_in, place_ref, local_sem.at[2])
    load_tissue = pltpu.make_async_copy(tissue_in, tissue_ref, local_sem.at[3])
    load_j.start()
    load_i.start()
    load_place.start()
    load_tissue.start()
    pl.semaphore_wait(barrier, len(along_y) + len(along_x) + len(next_z))

    up, down = along_y[1], along_y[2]
    halos = []
    for index, (source, target, peer) in enumerate(
        (
            (fixed_hbm.at[0, 4:8], halo_i.at[0], up),
            (fixed_hbm.at[0, 0:4], halo_i.at[1], down),
            (moving_hbm.at[0, 4:8], halo_j.at[0, 1:5], up),
            (moving_hbm.at[0, 0:4], halo_j.at[1, 0:4], down),
            (moving_hbm.at[0, 3:4], halo_j.at[0, 0:1], up),
            (moving_hbm.at[0, 4:5], halo_j.at[1, 4:5], down),
        )
    ):
        copy = pltpu.make_async_remote_copy(
            source, target, halo_send.at[index], halo_recv.at[index],
            device_id=peer, device_id_type=MESH,
        )
        copy.start()
        halos.append(copy)
    def tell(index):
        for d in (ROUNDS[index], -ROUNDS[index]):
            pl.semaphore_signal(known.at[index], inc=1, device_id=along_z[d], device_id_type=MESH)

    tell(0)

    r, c = iota((256, 256), 0), iota((256, 256), 1)
    same = (r >> 5) == (c >> 5)
    box_rows[...] = jnp.where(same & (jnp.abs(r - c) <= 4), 1.0, 0.0).astype(BF16)
    grad_rows[...] = jnp.where(
        same & (c - r == 1), 0.5, jnp.where(same & (r - c == 1), -0.5, 0.0)
    ).astype(BF16)
    r, c = iota((128, 128), 0), iota((128, 128), 1)
    band = jnp.where(jnp.abs(r - c) <= 4, 1.0, 0.0).astype(BF16)
    box_cols[0:128, :] = band
    box_cols[128:256, :] = band
    grad_cols[...] = jnp.where(r - c == 1, 0.5, jnp.where(c - r == 1, -0.5, 0.0)).astype(BF16)
    turn = lane_parts((128, 128))[1] - 1
    weight = jnp.zeros((128, 128), F32)
    for step, share in ((-1, 0.25), (0, 0.5), (1, 0.25)):
        b = turn + step
        weight = weight + jnp.where((b >= 0) & (b < 8), share * group_weight(r - 16 * b), 0.0)
    high, low = split(weight)
    gauss_cols[0:128, :] = high
    gauss_cols[128:256, :] = high
    gauss_cols[256:384, :] = low

    inside_low = jnp.where(gz > 0, 1.0, 0.0)
    inside_high = jnp.where(gz < NY - 1, 1.0, 0.0)
    load_j.wait()
    load_i.wait()
    load_place.wait()
    load_tissue.wait()
    for p in range(8):
        image_i[4 + p] = own_i[p].astype(F32)
        image_j[5 + p] = own_j[p].astype(F32)
    flat = own_j[...].reshape(256, 128)
    slope_x[128:384, :] = jnp.dot(grad_rows[...], flat, preferred_element_type=F32)
    slope_y[128:384, :] = jnp.dot(flat, grad_cols[...], preferred_element_type=F32)

    def box_sums(slot):
        field = jnp.dot(box_rows[...], sums[slot], preferred_element_type=F32)
        high, low = split(field[:, :128] + field[:, 128:])
        field = jnp.dot(
            jnp.concatenate([high, low], axis=1), box_cols[...], preferred_element_type=F32
        )
        return field * (1.0 / 729.0)

    def products(fixed, moved):
        return (
            fixed,
            [a * a for a in fixed],
            moved,
            [b * b for b in moved],
            [a * b for a, b in zip(fixed, moved)],
        )

    def put_sums(slot, chunk, inner, outer):
        for p in range(8):
            high, low = split(inner[p] + outer[p])
            at = pl.ds(32 * p + 16 * chunk, 16)
            sums[slot, at, 0:128] = high
            sums[slot, at, 128:256] = low

    for chunk in range(2):
        at = pl.ds(16 * chunk, 16)
        fixed = [image_i[4 + p, at, :] for p in range(8)]
        moved = [image_j[5 + p, at, :] for p in range(8)]
        for slot, planes in enumerate(products(fixed, moved)):
            for p, value in enumerate(own_sums(planes)):
                inner_sums[slot, p, at, :] = value

    pl.semaphore_wait(known.at[0], 2)
    tell(1)
    pl.semaphore_wait(known.at[1], 2)
    tell(2)

    for copy in halos[:2]:
        copy.wait_recv()
    for p in range(4):
        image_i[p] = halo_i[0, p].astype(F32) * inside_low
        image_i[12 + p] = halo_i[1, p].astype(F32) * inside_high

    depth_weight = []
    for p in range(8):
        at = gz * 8 + p
        first = group_weight(at)
        second = group_weight(at - 16)
        depth_weight.append((0.5 * first + 0.25 * second, 0.25 * first + 0.5 * second))
    lane = iota((32, 128), 1)
    lane_group, lane_turn = lane_parts((32, 128))
    row_weight = group_weight(iota((32, 128), 0) - 16 * (lane >> 6))
    place = place_ref[0]
    tissue = tissue_ref[0].astype(F32)

    def piece(images, first):
        totals = [None] * 6
        for p in range(8):
            at = pl.ds(32 * p, 32)
            mean_i, var_i = stat_i[0, at, :], stat_i[1, at, :]
            mean_w = means[0, at, :]
            var_w = means[1, at, :] - mean_w * mean_w
            cov = means[2, at, :] - mean_i * mean_w
            denom = var_i * var_w + EPSILON
            ratio = cov / denom
            if not first:
                cc_ref[0, p] = cov * ratio
            image = image_i[4 + p]
            mid = images[4 + p]
            dcc = 2.0 * ratio * (image - mean_i - cov / (var_w + EPSILON) * (mid - mean_w))
            if first:
                along_rows = slope_x[128 + 32 * p : 160 + 32 * p, :]
                along_cols = slope_y[128 + 32 * p : 160 + 32 * p, :]
            else:
                along_rows = 0.5 * (shifted(mid, -1, 0) - shifted(mid, 1, 0))
                along_cols = 0.5 * (shifted(mid, -1, 1) - shifted(mid, 1, 1))
            along_depth = 0.5 * (images[5 + p] - images[3 + p])
            for c, slope in enumerate((along_depth, along_rows, along_cols)):
                force = dcc * slope
                for k in range(2):
                    term = depth_weight[p][k] * force
                    totals[2 * c + k] = term if p == 0 else totals[2 * c + k] + term
        stack = []
        for ck in range(6):
            high, low = split(totals[ck])
            stack.append(jnp.concatenate([high, low, high], axis=1))
        parts = jnp.dot(
            jnp.concatenate(stack, axis=0), gauss_cols[...], preferred_element_type=F32
        )
        merged = jnp.zeros((32, 128), F32)
        for ck in range(6):
            merged = jnp.where(lane_group == ck, parts[32 * ck : 32 * ck + 32], merged)
        row = jnp.sum(merged * row_weight, axis=0, keepdims=True) * tissue
        lane_row = iota((1, 128), 1)
        return jnp.where(lane_row == PLACE_LANE, place.astype(F32) * 0.25, row)

    unsent = []

    def exchange(source, targets, sem, partners):
        for index, peer in enumerate(partners):
            pltpu.make_async_remote_copy(
                source, targets.at[index], gather_send.at[sem], gather_recv.at[sem],
                device_id=peer, device_id_type=MESH,
            ).start()
        done = pltpu.make_async_remote_copy(
            targets, targets, gather_send.at[sem], gather_recv.at[sem],
            device_id=partners[0], device_id_type=MESH,
        )
        unsent.append(done)
        return done

    def start_gather(turn, row):
        rows_y[turn, 0] = row
        summed = exchange(rows_y.at[turn, 0], rows_y.at[turn, 1:NY], 2 * turn, along_y)
        waits = [exchange(rows_y.at[turn, 0], unsummed, 4, opposite)] if turn == 1 else []
        skip = OPPOSITE if turn == 1 else 0
        if turn == 0:
            pl.semaphore_wait(known.at[2], 2)
            tell(3)
        summed.wait_recv()
        every = rows.at[turn]
        rows[turn, 0] = (rows_y[turn, 0] + rows_y[turn, 1]) + (rows_y[turn, 2] + rows_y[turn, 3])
        if turn == 0:
            pl.semaphore_wait(known.at[3], 2)
        done = exchange(every.at[0], every.at[1 + skip : 128], 2 * turn + 1, others[skip:])
        return [done] + waits

    def finish_gather(turn, waits):
        for done in waits:
            done.wait_recv()
        if turn == 1:
            four = unsummed[...].reshape(OPPOSITE, NY, 1, 128)
            rows[turn, 1 : 1 + OPPOSITE] = (four[:, 0] + four[:, 2]) + (four[:, 1] + four[:, 3])
        return rows[turn].reshape(128, 128)

    def first_sums(slots):
        for chunk in range(2):
            at = pl.ds(16 * chunk, 16)
            fixed = [image_i[p, at, :] for p in (0, 1, 2, 3, 12, 13, 14, 15)]
            moved = [image_j[1 + p, at, :] for p in (0, 1, 2, 3, 12, 13, 14, 15)]
            for slot, planes in enumerate(products(fixed, moved)):
                if slot in slots:
                    inner = [inner_sums[slot, p, at, :] for p in range(8)]
                    put_sums(slot, chunk, inner, side_sums(planes[:4], planes[4:]))

    first_sums((0, 1))
    mean_i = box_sums(0)
    stat_i[0] = mean_i
    stat_i[1] = box_sums(1) - mean_i * mean_i
    for copy in halos[2:4]:
        copy.wait_recv()
    for p in range(4):
        image_j[1 + p] = halo_j[0, 1 + p].astype(F32) * inside_low
        image_j[13 + p] = halo_j[1, p].astype(F32) * inside_high
    first_sums((2, 3, 4))
    for slot in range(3):
        means[slot] = box_sums(2 + slot)
    row = piece([image_j[1 + p] for p in range(16)], True)
    waits = start_gather(0, row)

    own_row, own_col = place >> 3, place & 7
    r, c = iota((128, 128), 0), iota((128, 128), 1)
    inner = (own_col * 128 + c).astype(F32)
    inner = jnp.clip((inner + 0.5) * (1.0 / 16.0) - 0.5, 0.0, 63.0)
    turn = (r & 63) - WIDE * (((r & 63) * 205) >> 11) - 1
    for first_row, col in ((0, own_col - jnp.where(r < 64, 1, 0)), (256, own_col + 1)):
        gap = inner - (8 * col + turn).astype(F32)
        weight = jnp.maximum(0.0, 1.0 - jnp.abs(gap)).astype(BF16)
        to_cols[first_row : first_row + 128, :] = weight
        if first_row == 0:
            to_cols[128:256, :] = weight

    for copy in halos[4:]:
        copy.wait_recv()
    image_j[0] = halo_j[0, 0].astype(F32) * inside_low
    image_j[17] = halo_j[1, 4].astype(F32) * inside_high
    for start, side, offset in ((0, 0, 1), (384, 1, 0)):
        flat = halo_j[side, offset : offset + 4].reshape(128, 128)
        slope_x[start : start + 128, :] = jnp.dot(
            grad_rows[0:128, 0:128], flat, preferred_element_type=F32
        )
        slope_y[start : start + 128, :] = jnp.dot(
            flat, grad_cols[...], preferred_element_type=F32
        )

    gathered = finish_gather(0, waits)

    spot = jnp.broadcast_to(gathered[:, PLACE_LANE : PLACE_LANE + 1], (128, 128))
    r, c = iota((128, 128), 0), iota((128, 128), 1)
    spot = jnp.sum(jnp.where(r == c, spot, 0.0), axis=0, keepdims=True).astype(jnp.int32)
    mark = ((spot >> 3) * 2).astype(F32)
    mark = jnp.broadcast_to(jnp.concatenate([mark, mark + 1.0], axis=1), (32, 256))
    spot_col = jnp.broadcast_to(jnp.concatenate([spot & 7, spot & 7], axis=1), (32, 256))
    at = iota((32, 256), 0)
    filtered = hat_tri(at.astype(F32), mark)
    inner = (own_row * 32 + at).astype(F32)
    inner = hat_tri(jnp.clip((inner + 0.5) * (1.0 / 16.0) - 0.5, 0.0, 31.0), mark)
    for d in range(3):
        value = jnp.where(spot_col == own_col + (d - 1), inner, 0.0)
        combine[32 * d : 32 * d + 32, :] = value.astype(BF16)
    for col in range(8):
        value = jnp.where(spot_col == col, filtered, 0.0)
        combine[96 + 32 * col : 128 + 32 * col, :] = value.astype(BF16)

    first_half = iota((128, 128), 1) < 64
    groups, turns = lane_parts((32, 128))

    def combined(gathered, start):
        turned = pltpu.roll(gathered, 64, 1)
        right = lambda high, low: jnp.where(first_half, high, low - low.astype(BF16).astype(F32))
        both = jnp.concatenate([right(gathered, turned), right(turned, gathered)], axis=0)
        return jnp.dot(combine[start:352, :], both.astype(BF16), preferred_element_type=F32)

    def regular_of(grid):
        low_lanes = first_half[0:16]
        cols = []
        for col in range(8):
            top, bottom = grid[32 * col : 32 * col + 16], grid[32 * col + 16 : 32 * col + 32]
            cols.append(
                jnp.where(low_lanes, top, bottom)
                + pltpu.roll(jnp.where(low_lanes, bottom, top), 64, 1)
            )
        out = []
        squares = jnp.zeros((16, 128), F32)
        group, turn = groups[0:16], turns[0:16]
        inside = (turn >= 1) & (turn <= 8) & (group < 6)
        for col in range(8):
            value = cols[col]
            if col > 0:
                value = value + jnp.where(turn == 1, pltpu.roll(cols[col - 1], 120, 1), 0.0)
            if col < 7:
                value = value + jnp.where(turn == 8, pltpu.roll(cols[col + 1], 8, 1), 0.0)
            value = jnp.where(inside, value, 0.0)
            squares = squares + value * value
            out.append(value)
        mean = jnp.sum(squares, keepdims=True) * (1.0 / (6 * 32 * 64))
        return out, STEP_LENGTH / jnp.sqrt(mean + EPSILON)

    grid = combined(gathered, 0)
    around = grid[0:96] + pltpu.roll(grid[0:96], 64, 1)
    half = first_half[0:32]
    near = jnp.where(half, around[0:32], around[32:64])
    high, low = split(near)
    above_high, above_low = split(around[64:96])
    above = jnp.where(half, above_high.astype(F32), above_low.astype(F32)).astype(BF16)
    wide = jnp.concatenate([high, low, above], axis=1)
    group_wide = jnp.concatenate([groups, groups, groups], axis=1)
    stack = [jnp.where(group_wide == ck, wide, jnp.zeros_like(wide)) for ck in range(6)]
    moves = jnp.dot(jnp.concatenate(stack, axis=0), to_cols[...], preferred_element_type=F32)
    regular, scale = regular_of(grid[96:352])
    for col in range(8):
        before[col] = regular[col] * scale
    shift = []
    for c in range(3):
        value, other = moves[64 * c : 64 * c + 32], moves[64 * c + 32 : 64 * c + 64]
        shift.append((value, other - value))

    for p in range(16):
        deep = (gz * 8 + (p - 4)).astype(F32)
        part = jnp.clip((deep + 0.5) * (1.0 / 16.0) - 0.5, 0.0, 1.0)
        slopes = (
            0.5 * (image_j[2 + p] - image_j[p]),
            slope_x[32 * p : 32 * p + 32, :],
            slope_y[32 * p : 32 * p + 32, :],
        )
        change = sum((base + part * rise) * slope for (base, rise), slope in zip(shift, slopes))
        value = image_j[1 + p] + scale * change
        if p < 4:
            value = value * inside_low
        if p >= 12:
            value = value * inside_high
        warped_ref[p] = value
    for chunk in range(2):
        at = pl.ds(16 * chunk, 16)
        fixed = [image_i[p, at, :] for p in range(16)]
        moved = [warped_ref[p, at, :] for p in range(16)]
        for slot, planes in enumerate(products(fixed, moved)):
            if slot >= 2:
                put_sums(
                    slot, chunk, own_sums(planes[4:12]), side_sums(planes[0:4], planes[12:16])
                )
    for slot in range(3):
        means[slot] = box_sums(2 + slot)
    row = piece([warped_ref[p] for p in range(16)], False)
    waits = start_gather(1, row)
    regular, scale = regular_of(combined(finish_gather(1, waits), 96))
    total = [before[col] + regular[col] * scale for col in range(8)]
    lane_col = (iota((16, 128), 1) >> 3) & 7
    for ck in range(6):
        value = jnp.zeros((16, 128), F32)
        for col in range(8):
            moved = pltpu.roll(total[col], (8 * col - WIDE * ck - 1) % 128, 1)
            value = jnp.where(lane_col == col, moved, value)
        velocity_ref[ck // 2, ck % 2, 0:16, :] = value[:, 0:64]
        velocity_ref[ck // 2, ck % 2, 16:32, :] = value[:, 64:128]
    for copy in halos:
        copy.wait_send()
    for copy in unsent:
        copy.wait_send()


def per_device(fixed, moving, block_place, tissue):
    vmem = pltpu.VMEM
    return pl.pallas_call(
        kernel,
        out_shape=(
            jax.ShapeDtypeStruct((3, 2, 32, 64), F32),
            jax.ShapeDtypeStruct((1, 8, 32, 128), F32),
        ),
        in_specs=[
            pl.BlockSpec(memory_space=pltpu.HBM),
            pl.BlockSpec(memory_space=pltpu.HBM),
            pl.BlockSpec(memory_space=pltpu.HBM),
            pl.BlockSpec(memory_space=pltpu.HBM),
        ],
        out_specs=(
            pl.BlockSpec(memory_space=pltpu.VMEM),
            pl.BlockSpec(memory_space=pltpu.VMEM),
        ),
        scratch_shapes=[
            vmem((8, 32, 128), BF16),
            vmem((8, 32, 128), BF16),
            vmem((2, 4, 32, 128), BF16),
            vmem((2, 5, 32, 128), BF16),
            vmem((16, 32, 128), F32),
            vmem((18, 32, 128), F32),
            vmem((512, 128), F32),
            vmem((512, 128), F32),
            vmem((16, 32, 128), F32),
            vmem((256, 256), BF16),
            vmem((256, 128), BF16),
            vmem((256, 256), BF16),
            vmem((128, 128), BF16),
            vmem((384, 128), BF16),
            vmem((384, 128), BF16),
            vmem((5, 8, 32, 128), F32),
            vmem((5, 256, 256), BF16),
            vmem((3, 256, 128), F32),
            vmem((2, 256, 128), F32),
            vmem((352, 256), BF16),
            vmem((8, 16, 128), F32),
            vmem((2, NY, 1, 128), F32),
            vmem((2, 128, 1, 128), F32),
            vmem((OPPOSITE * NY, 1, 128), F32),
            pltpu.SMEM((1,), jnp.int32),
            pltpu.SMEM((1,), jnp.int32),
            pltpu.SemaphoreType.DMA((4,)),
            pltpu.SemaphoreType.DMA((6,)),
            pltpu.SemaphoreType.DMA((6,)),
            pltpu.SemaphoreType.DMA((5,)),
            pltpu.SemaphoreType.DMA((5,)),
            pltpu.SemaphoreType.REGULAR((len(ROUNDS),)),
        ],
        compiler_params=pltpu.CompilerParams(
            collective_id=0, has_side_effects=True, vmem_limit_bytes=32 * 1024 * 1024
        ),
    )(
        pltpu.with_memory_space_constraint(fixed, pltpu.HBM),
        pltpu.with_memory_space_constraint(moving, pltpu.HBM),
        block_place,
        tissue,
    )


def solution(mesh):
    return jax.shard_map(
        per_device,
        mesh=mesh,
        in_specs=(P("blk", "gz", None, None), P("blk", "gz", None, None), P("blk"), P("blk")),
        out_specs=(P(), P("blk", "gz", None, None)),
        check_vma=False,
    )
```

```python
import functools
import math

import jax
import jax.numpy as jnp
from jax import lax
from jax.experimental import pallas as pl
from jax.experimental.pallas import tpu as pltpu
from jax.sharding import PartitionSpec as P

NX, NY, NZC = 4, 4, 16
F32, BF16 = jnp.float32, jnp.bfloat16
EPSILON = 1e-05
STEP_LENGTH = 0.5
RAW = [math.exp(-(t * t) / 4.5) for t in range(4)]
TOTAL = RAW[0] + 2 * (RAW[1] + RAW[2] + RAW[3])
W1, W2, W3 = (RAW[t] / TOTAL for t in (1, 2, 3))
WIDE = 10
PLACE_LANE = 60
MESH = pl.DeviceIdType.MESH
OPPOSITE = 2 * NX
ROUNDS = (1, 2, 4, 1)


def coordinates():
    blk = lax.axis_index("blk")
    return blk // (2 * NZC), lax.axis_index("gz"), (blk // 2) % NZC, blk % 2


def far_first():
    steps = [(z, x, c) for z in range(NZC) for x in range(NX) for c in range(2)][1:]
    return sorted(steps, key=lambda s: -(4 * min(s[0], NZC - s[0]) + min(s[1], NX - s[1]) + 0.3 * s[2]))


def peers():
    x, y, z, core = coordinates()
    at_x = [(x + d) % NX * (2 * NZC) for d in range(NX)]
    at_z = [(z + d) % NZC * 2 for d in range(NZC)]
    at_core = [core, 1 - core]
    base = x * (2 * NZC) + z * 2 + core
    along_y = [(base, (y + d) % NY) for d in (2, 1, 3)]
    along_x = [(at_x[d // 2] + at_z[0] + at_core[d % 2], y) for d in range(1, 2 * NX)]
    along_z = {d: (at_x[0] + at_z[d % NZC] + core, y) for d in (1, 2, 4, -1, -2, -4)}
    others = [(at_x[dx] + at_z[dz] + at_core[dc], y) for dz, dx, dc in far_first()]
    opposite = [(peer, (y + d) % NY) for peer, _ in others[:OPPOSITE] for d in range(NY)]
    return along_y, along_x, along_z, others, opposite


def iota(shape, dim):
    return lax.broadcasted_iota(jnp.int32, shape, dim)


def lane_parts(shape):
    lane = iota(shape, len(shape) - 1) & 63
    group = (lane * 205) >> 11
    return group, lane - WIDE * group


def split(value):
    high = value.astype(BF16)
    return high, (value - high.astype(F32)).astype(BF16)


def group_weight(t):
    near = jnp.minimum(t, 15 - t)
    out = jnp.where(near >= 3, 1.0, 0.0)
    for at, value in (
        (2, 1 - W3),
        (1, 1 - W3 - W2),
        (0, 1 - W3 - W2 - W1),
        (-1, W1 + W2 + W3),
        (-2, W2 + W3),
        (-3, W3),
    ):
        out = jnp.where(near == at, value, out)
    return out


def hat_tri(where, mark):
    gap = where - mark
    hat = lambda d: jnp.maximum(0.0, 1.0 - jnp.abs(d))
    return 0.5 * hat(gap) + 0.25 * (hat(gap - 1.0) + hat(gap + 1.0))


def own_sums(a):
    mid = a[3] + a[4]
    out0 = (a[0] + a[1]) + (a[2] + mid)
    out1 = out0 + a[5]
    out2 = out1 + a[6]
    out3 = out2 + a[7]
    out7 = mid + (a[5] + (a[6] + a[7]))
    out6 = out7 + a[2]
    out5 = out6 + a[1]
    return [out0, out1, out2, out3, out3, out5, out6, out7]


def side_sums(low, high):
    out3 = low[3]
    out2 = low[2] + out3
    out1 = low[1] + out2
    out0 = low[0] + out1
    out4 = high[0]
    out5 = out4 + high[1]
    out6 = out5 + high[2]
    out7 = out6 + high[3]
    return [out0, out1, out2, out3, out4, out5, out6, out7]


def shifted(value, amount, dim):
    size = value.shape[dim]
    at = iota(value.shape, dim)
    edge = 0 if amount == 1 else size - 1
    return jnp.where(at == edge, 0.0, pltpu.roll(value, amount % size, dim))


def kernel(
    fixed_hbm, moving_hbm, place_in, tissue_in,
    velocity_ref, cc_ref,
    own_i, own_j, halo_i, halo_j,
    image_i, image_j, slope_x, slope_y, warped_ref,
    box_rows, box_cols, grad_rows, grad_cols, gauss_cols, to_cols,
    inner_sums, sums, means, stat_i, combine, before,
    rows_y, rows, unsummed, place_ref, tissue_ref, local_sem, halo_send, halo_recv, gather_send, gather_recv, known,
):
    gz = lax.axis_index("gz")
    along_y, along_x, along_z, others, opposite = peers()
    next_z = [along_z[1], along_z[-1]]
    barrier = pltpu.get_barrier_semaphore()
    for peer in along_y + along_x + next_z:
        pl.semaphore_signal(barrier, inc=1, device_id=peer, device_id_type=MESH)
    load_j = pltpu.make_async_copy(moving_hbm.at[0], own_j, local_sem.at[0])
    load_i = pltpu.make_async_copy(fixed_hbm.at[0], own_i, local_sem.at[1])
    load_place = pltpu.make_async_copy(place_in, place_ref, local_sem.at[2])
    load_tissue = pltpu.make_async_copy(tissue_in, tissue_ref, local_sem.at[3])
    load_j.start()
    load_i.start()
    load_place.start()
    load_tissue.start()
    pl.semaphore_wait(barrier, len(along_y) + len(along_x) + len(next_z))

    up, down = along_y[1], along_y[2]
    halos = []
    for index, (source, target, peer) in enumerate(
        (
            (fixed_hbm.at[0, 4:8], halo_i.at[0], up),
            (fixed_hbm.at[0, 0:4], halo_i.at[1], down),
            (moving_hbm.at[0, 4:8], halo_j.at[0, 1:5], up),
            (moving_hbm.at[0, 0:4], halo_j.at[1, 0:4], down),
            (moving_hbm.at[0, 3:4], halo_j.at[0, 0:1], up),
            (moving_hbm.at[0, 4:5], halo_j.at[1, 4:5], down),
        )
    ):
        copy = pltpu.make_async_remote_copy(
            source, target, halo_send.at[index], halo_recv.at[index],
            device_id=peer, device_id_type=MESH,
        )
        copy.start()
        halos.append(copy)
    def tell(index):
        for d in (ROUNDS[index], -ROUNDS[index]):
            pl.semaphore_signal(known.at[index], inc=1, device_id=along_z[d], device_id_type=MESH)

    tell(0)

    r, c = iota((256, 256), 0), iota((256, 256), 1)
    same = (r >> 5) == (c >> 5)
    box_rows[...] = jnp.where(same & (jnp.abs(r - c) <= 4), 1.0, 0.0).astype(BF16)
    grad_rows[...] = jnp.where(
        same & (c - r == 1), 0.5, jnp.where(same & (r - c == 1), -0.5, 0.0)
    ).astype(BF16)
    r, c = iota((128, 128), 0), iota((128, 128), 1)
    band = jnp.where(jnp.abs(r - c) <= 4, 1.0, 0.0).astype(BF16)
    box_cols[0:128, :] = band
    box_cols[128:256, :] = band
    grad_cols[...] = jnp.where(r - c == 1, 0.5, jnp.where(c - r == 1, -0.5, 0.0)).astype(BF16)
    turn = lane_parts((128, 128))[1] - 1
    weight = jnp.zeros((128, 128), F32)
    for step, share in ((-1, 0.25), (0, 0.5), (1, 0.25)):
        b = turn + step
        weight = weight + jnp.where((b >= 0) & (b < 8), share * group_weight(r - 16 * b), 0.0)
    high, low = split(weight)
    gauss_cols[0:128, :] = high
    gauss_cols[128:256, :] = high
    gauss_cols[256:384, :] = low

    inside_low = jnp.where(gz > 0, 1.0, 0.0)
    inside_high = jnp.where(gz < NY - 1, 1.0, 0.0)
    pl.semaphore_wait(known.at[0], 2)
    tell(1)
    load_j.wait()
    load_i.wait()
    load_place.wait()
    load_tissue.wait()
    for p in range(8):
        image_i[4 + p] = own_i[p].astype(F32)
        image_j[5 + p] = own_j[p].astype(F32)
    flat = own_j[...].reshape(256, 128)
    slope_x[128:384, :] = jnp.dot(grad_rows[...], flat, preferred_element_type=F32)
    slope_y[128:384, :] = jnp.dot(flat, grad_cols[...], preferred_element_type=F32)

    def box_sums(slot):
        field = jnp.dot(box_rows[...], sums[slot], preferred_element_type=F32)
        high, low = split(field[:, :128] + field[:, 128:])
        field = jnp.dot(
            jnp.concatenate([high, low], axis=1), box_cols[...], preferred_element_type=F32
        )
        return field * (1.0 / 729.0)

    def products(fixed, moved):
        return (
            fixed,
            [a * a for a in fixed],
            moved,
            [b * b for b in moved],
            [a * b for a, b in zip(fixed, moved)],
        )

    def put_sums(slot, chunk, inner, outer):
        for p in range(8):
            high, low = split(inner[p] + outer[p])
            at = pl.ds(32 * p + 16 * chunk, 16)
            sums[slot, at, 0:128] = high
            sums[slot, at, 128:256] = low

    for chunk in range(2):
        at = pl.ds(16 * chunk, 16)
        fixed = [image_i[4 + p, at, :] for p in range(8)]
        moved = [image_j[5 + p, at, :] for p in range(8)]
        for slot, planes in enumerate(products(fixed, moved)):
            for p, value in enumerate(own_sums(planes)):
                inner_sums[slot, p, at, :] = value

    pl.semaphore_wait(known.at[1], 2)
    tell(2)

    for copy in halos[:2]:
        copy.wait_recv()
    for p in range(4):
        image_i[p] = halo_i[0, p].astype(F32) * inside_low
        image_i[12 + p] = halo_i[1, p].astype(F32) * inside_high

    depth_weight = []
    for p in range(8):
        at = gz * 8 + p
        first = group_weight(at)
        second = group_weight(at - 16)
        depth_weight.append((0.5 * first + 0.25 * second, 0.25 * first + 0.5 * second))
    lane = iota((32, 128), 1)
    lane_group, lane_turn = lane_parts((32, 128))
    row_weight = group_weight(iota((32, 128), 0) - 16 * (lane >> 6))
    place = place_ref[0]
    tissue = tissue_ref[0].astype(F32)

    def piece(images, first):
        totals = [None] * 6
        for p in range(8):
            at = pl.ds(32 * p, 32)
            mean_i, var_i = stat_i[0, at, :], stat_i[1, at, :]
            mean_w = means[0, at, :]
            var_w = means[1, at, :] - mean_w * mean_w
            cov = means[2, at, :] - mean_i * mean_w
            denom = var_i * var_w + EPSILON
            ratio = cov / denom
            if not first:
                cc_ref[0, p] = cov * ratio
            image = image_i[4 + p]
            mid = images[4 + p]
            dcc = 2.0 * ratio * (image - mean_i - cov / (var_w + EPSILON) * (mid - mean_w))
            if first:
                along_rows = slope_x[128 + 32 * p : 160 + 32 * p, :]
                along_cols = slope_y[128 + 32 * p : 160 + 32 * p, :]
            else:
                along_rows = 0.5 * (shifted(mid, -1, 0) - shifted(mid, 1, 0))
                along_cols = 0.5 * (shifted(mid, -1, 1) - shifted(mid, 1, 1))
            along_depth = 0.5 * (images[5 + p] - images[3 + p])
            for c, slope in enumerate((along_depth, along_rows, along_cols)):
                force = dcc * slope
                for k in range(2):
                    term = depth_weight[p][k] * force
                    totals[2 * c + k] = term if p == 0 else totals[2 * c + k] + term
        stack = []
        for ck in range(6):
            high, low = split(totals[ck])
            stack.append(jnp.concatenate([high, low, high], axis=1))
        parts = jnp.dot(
            jnp.concatenate(stack, axis=0), gauss_cols[...], preferred_element_type=F32
        )
        merged = jnp.zeros((32, 128), F32)
        for ck in range(6):
            merged = jnp.where(lane_group == ck, parts[32 * ck : 32 * ck + 32], merged)
        row = jnp.sum(merged * row_weight, axis=0, keepdims=True) * tissue
        lane_row = iota((1, 128), 1)
        return jnp.where(lane_row == PLACE_LANE, place.astype(F32) * 0.25, row)

    unsent = []

    def exchange(source, targets, sem, partners):
        for index, peer in enumerate(partners):
            pltpu.make_async_remote_copy(
                source, targets.at[index], gather_send.at[sem], gather_recv.at[sem],
                device_id=peer, device_id_type=MESH,
            ).start()
        done = pltpu.make_async_remote_copy(
            targets, targets, gather_send.at[sem], gather_recv.at[sem],
            device_id=partners[0], device_id_type=MESH,
        )
        unsent.append(done)
        return done

    def start_gather(turn, row):
        rows_y[turn, 0] = row
        summed = exchange(rows_y.at[turn, 0], rows_y.at[turn, 1:NY], 2 * turn, along_y)
        waits = [exchange(rows_y.at[turn, 0], unsummed, 4, opposite)] if turn == 1 else []
        skip = OPPOSITE if turn == 1 else 0
        if turn == 0:
            pl.semaphore_wait(known.at[2], 2)
            tell(3)
        summed.wait_recv()
        every = rows.at[turn]
        rows[turn, 0] = (rows_y[turn, 0] + rows_y[turn, 1]) + (rows_y[turn, 2] + rows_y[turn, 3])
        if turn == 0:
            pl.semaphore_wait(known.at[3], 2)
        done = exchange(every.at[0], every.at[1 + skip : 128], 2 * turn + 1, others[skip:])
        return [done] + waits

    def finish_gather(turn, waits):
        for done in waits:
            done.wait_recv()
        if turn == 1:
            four = unsummed[...].reshape(OPPOSITE, NY, 1, 128)
            rows[turn, 1 : 1 + OPPOSITE] = (four[:, 0] + four[:, 2]) + (four[:, 1] + four[:, 3])
        return rows[turn].reshape(128, 128)

    def first_sums(slots):
        for chunk in range(2):
            at = pl.ds(16 * chunk, 16)
            fixed = [image_i[p, at, :] for p in (0, 1, 2, 3, 12, 13, 14, 15)]
            moved = [image_j[1 + p, at, :] for p in (0, 1, 2, 3, 12, 13, 14, 15)]
            for slot, planes in enumerate(products(fixed, moved)):
                if slot in slots:
                    inner = [inner_sums[slot, p, at, :] for p in range(8)]
                    put_sums(slot, chunk, inner, side_sums(planes[:4], planes[4:]))

    first_sums((0, 1))
    mean_i = box_sums(0)
    stat_i[0] = mean_i
    stat_i[1] = box_sums(1) - mean_i * mean_i
    for copy in halos[2:4]:
        copy.wait_recv()
    for p in range(4):
        image_j[1 + p] = halo_j[0, 1 + p].astype(F32) * inside_low
        image_j[13 + p] = halo_j[1, p].astype(F32) * inside_high
    first_sums((2, 3, 4))
    for slot in range(3):
        means[slot] = box_sums(2 + slot)
    row = piece([image_j[1 + p] for p in range(16)], True)
    waits = start_gather(0, row)

    own_row, own_col = place >> 3, place & 7
    r, c = iota((128, 128), 0), iota((128, 128), 1)
    inner = (own_col * 128 + c).astype(F32)
    inner = jnp.clip((inner + 0.5) * (1.0 / 16.0) - 0.5, 0.0, 63.0)
    turn = (r & 63) - WIDE * (((r & 63) * 205) >> 11) - 1
    for first_row, col in ((0, own_col - jnp.where(r < 64, 1, 0)), (256, own_col + 1)):
        gap = inner - (8 * col + turn).astype(F32)
        weight = jnp.maximum(0.0, 1.0 - jnp.abs(gap)).astype(BF16)
        to_cols[first_row : first_row + 128, :] = weight
        if first_row == 0:
            to_cols[128:256, :] = weight

    for copy in halos[4:]:
        copy.wait_recv()
    image_j[0] = halo_j[0, 0].astype(F32) * inside_low
    image_j[17] = halo_j[1, 4].astype(F32) * inside_high
    for start, side, offset in ((0, 0, 1), (384, 1, 0)):
        flat = halo_j[side, offset : offset + 4].reshape(128, 128)
        slope_x[start : start + 128, :] = jnp.dot(
            grad_rows[0:128, 0:128], flat, preferred_element_type=F32
        )
        slope_y[start : start + 128, :] = jnp.dot(
            flat, grad_cols[...], preferred_element_type=F32
        )

    gathered = finish_gather(0, waits)

    spot = jnp.broadcast_to(gathered[:, PLACE_LANE : PLACE_LANE + 1], (128, 128))
    r, c = iota((128, 128), 0), iota((128, 128), 1)
    spot = jnp.sum(jnp.where(r == c, spot, 0.0), axis=0, keepdims=True).astype(jnp.int32)
    mark = ((spot >> 3) * 2).astype(F32)
    mark = jnp.broadcast_to(jnp.concatenate([mark, mark + 1.0], axis=1), (32, 256))
    spot_col = jnp.broadcast_to(jnp.concatenate([spot & 7, spot & 7], axis=1), (32, 256))
    at = iota((32, 256), 0)
    filtered = hat_tri(at.astype(F32), mark)
    inner = (own_row * 32 + at).astype(F32)
    inner = hat_tri(jnp.clip((inner + 0.5) * (1.0 / 16.0) - 0.5, 0.0, 31.0), mark)
    for d in range(3):
        value = jnp.where(spot_col == own_col + (d - 1), inner, 0.0)
        combine[32 * d : 32 * d + 32, :] = value.astype(BF16)
    for col in range(8):
        value = jnp.where(spot_col == col, filtered, 0.0)
        combine[96 + 32 * col : 128 + 32 * col, :] = value.astype(BF16)

    first_half = iota((128, 128), 1) < 64
    groups, turns = lane_parts((32, 128))

    def combined(gathered, start):
        turned = pltpu.roll(gathered, 64, 1)
        right = lambda high, low: jnp.where(first_half, high, low - low.astype(BF16).astype(F32))
        both = jnp.concatenate([right(gathered, turned), right(turned, gathered)], axis=0)
        return jnp.dot(combine[start:352, :], both.astype(BF16), preferred_element_type=F32)

    def regular_of(grid):
        low_lanes = first_half[0:16]
        cols = []
        for col in range(8):
            top, bottom = grid[32 * col : 32 * col + 16], grid[32 * col + 16 : 32 * col + 32]
            cols.append(
                jnp.where(low_lanes, top, bottom)
                + pltpu.roll(jnp.where(low_lanes, bottom, top), 64, 1)
            )
        out = []
        squares = jnp.zeros((16, 128), F32)
        group, turn = groups[0:16], turns[0:16]
        inside = (turn >= 1) & (turn <= 8) & (group < 6)
        for col in range(8):
            value = cols[col]
            if col > 0:
                value = value + jnp.where(turn == 1, pltpu.roll(cols[col - 1], 120, 1), 0.0)
            if col < 7:
                value = value + jnp.where(turn == 8, pltpu.roll(cols[col + 1], 8, 1), 0.0)
            value = jnp.where(inside, value, 0.0)
            squares = squares + value * value
            out.append(value)
        mean = jnp.sum(squares, keepdims=True) * (1.0 / (6 * 32 * 64))
        return out, STEP_LENGTH / jnp.sqrt(mean + EPSILON)

    grid = combined(gathered, 0)
    around = grid[0:96] + pltpu.roll(grid[0:96], 64, 1)
    half = first_half[0:32]
    near = jnp.where(half, around[0:32], around[32:64])
    high, low = split(near)
    above_high, above_low = split(around[64:96])
    above = jnp.where(half, above_high.astype(F32), above_low.astype(F32)).astype(BF16)
    wide = jnp.concatenate([high, low, above], axis=1)
    group_wide = jnp.concatenate([groups, groups, groups], axis=1)
    stack = [jnp.where(group_wide == ck, wide, jnp.zeros_like(wide)) for ck in range(6)]
    moves = jnp.dot(jnp.concatenate(stack, axis=0), to_cols[...], preferred_element_type=F32)
    regular, scale = regular_of(grid[96:352])
    for col in range(8):
        before[col] = regular[col] * scale
    shift = []
    for c in range(3):
        value, other = moves[64 * c : 64 * c + 32], moves[64 * c + 32 : 64 * c + 64]
        shift.append((value, other - value))

    for p in range(16):
        deep = (gz * 8 + (p - 4)).astype(F32)
        part = jnp.clip((deep + 0.5) * (1.0 / 16.0) - 0.5, 0.0, 1.0)
        slopes = (
            0.5 * (image_j[2 + p] - image_j[p]),
            slope_x[32 * p : 32 * p + 32, :],
            slope_y[32 * p : 32 * p + 32, :],
        )
        change = sum((base + part * rise) * slope for (base, rise), slope in zip(shift, slopes))
        value = image_j[1 + p] + scale * change
        if p < 4:
            value = value * inside_low
        if p >= 12:
            value = value * inside_high
        warped_ref[p] = value
    for chunk in range(2):
        at = pl.ds(16 * chunk, 16)
        fixed = [image_i[p, at, :] for p in range(16)]
        moved = [warped_ref[p, at, :] for p in range(16)]
        for slot, planes in enumerate(products(fixed, moved)):
            if slot >= 2:
                put_sums(
                    slot, chunk, own_sums(planes[4:12]), side_sums(planes[0:4], planes[12:16])
                )
    for slot in range(3):
        means[slot] = box_sums(2 + slot)
    row = piece([warped_ref[p] for p in range(16)], False)
    waits = start_gather(1, row)
    regular, scale = regular_of(combined(finish_gather(1, waits), 96))
    total = [before[col] + regular[col] * scale for col in range(8)]
    lane_col = (iota((16, 128), 1) >> 3) & 7
    for ck in range(6):
        value = jnp.zeros((16, 128), F32)
        for col in range(8):
            moved = pltpu.roll(total[col], (8 * col - WIDE * ck - 1) % 128, 1)
            value = jnp.where(lane_col == col, moved, value)
        velocity_ref[ck // 2, ck % 2, 0:16, :] = value[:, 0:64]
        velocity_ref[ck // 2, ck % 2, 16:32, :] = value[:, 64:128]
    for copy in halos:
        copy.wait_send()
    for copy in unsent:
        copy.wait_send()


def per_device(fixed, moving, block_place, tissue):
    vmem = pltpu.VMEM
    return pl.pallas_call(
        kernel,
        out_shape=(
            jax.ShapeDtypeStruct((3, 2, 32, 64), F32),
            jax.ShapeDtypeStruct((1, 8, 32, 128), F32),
        ),
        in_specs=[
            pl.BlockSpec(memory_space=pltpu.HBM),
            pl.BlockSpec(memory_space=pltpu.HBM),
            pl.BlockSpec(memory_space=pltpu.HBM),
            pl.BlockSpec(memory_space=pltpu.HBM),
        ],
        out_specs=(
            pl.BlockSpec(memory_space=pltpu.VMEM),
            pl.BlockSpec(memory_space=pltpu.VMEM),
        ),
        scratch_shapes=[
            vmem((8, 32, 128), BF16),
            vmem((8, 32, 128), BF16),
            vmem((2, 4, 32, 128), BF16),
            vmem((2, 5, 32, 128), BF16),
            vmem((16, 32, 128), F32),
            vmem((18, 32, 128), F32),
            vmem((512, 128), F32),
            vmem((512, 128), F32),
            vmem((16, 32, 128), F32),
            vmem((256, 256), BF16),
            vmem((256, 128), BF16),
            vmem((256, 256), BF16),
            vmem((128, 128), BF16),
            vmem((384, 128), BF16),
            vmem((384, 128), BF16),
            vmem((5, 8, 32, 128), F32),
            vmem((5, 256, 256), BF16),
            vmem((3, 256, 128), F32),
            vmem((2, 256, 128), F32),
            vmem((352, 256), BF16),
            vmem((8, 16, 128), F32),
            vmem((2, NY, 1, 128), F32),
            vmem((2, 128, 1, 128), F32),
            vmem((OPPOSITE * NY, 1, 128), F32),
            pltpu.SMEM((1,), jnp.int32),
            pltpu.SMEM((1,), jnp.int32),
            pltpu.SemaphoreType.DMA((4,)),
            pltpu.SemaphoreType.DMA((6,)),
            pltpu.SemaphoreType.DMA((6,)),
            pltpu.SemaphoreType.DMA((5,)),
            pltpu.SemaphoreType.DMA((5,)),
            pltpu.SemaphoreType.REGULAR((len(ROUNDS),)),
        ],
        compiler_params=pltpu.CompilerParams(
            collective_id=0, has_side_effects=True, vmem_limit_bytes=32 * 1024 * 1024
        ),
    )(
        pltpu.with_memory_space_constraint(fixed, pltpu.HBM),
        pltpu.with_memory_space_constraint(moving, pltpu.HBM),
        block_place,
        tissue,
    )


def solution(mesh):
    return jax.shard_map(
        per_device,
        mesh=mesh,
        in_specs=(P("blk", "gz", None, None), P("blk", "gz", None, None), P("blk"), P("blk")),
        out_specs=(P(), P("blk", "gz", None, None)),
        check_vma=False,
    )
```
